128 devices in a mesh: seq: 16 (over y, x), fsdp: 8 (over z, core).
Axes of the slice: x: 4, y: 4, z: 4, core: 2. Of those that a mesh axis runs over, the one named last changes fastest.
Arguments:
- block_input: bfloat16 [2, 16384, 768], P(None, ('seq', 'fsdp')), may hold values from -6 to 6
- routes: int32 [2, 16384, 1], P(None, ('seq', 'fsdp')), may hold values from 0 to 7; in each aligned block of 128 rows (0 to 127, 128 to 255, ..., all dimensions but the last counted through in order) at most 20 rows name the same one
- cotangent: bfloat16 [2, 16384, 768], P(None, ('seq', 'fsdp')), may hold values from -6 to 6
- in_proj: bfloat16 [768, 3072], P(('seq', 'fsdp')), may hold values from -0.21875 to 0.21875
- conv_weight: bfloat16 [4, 1536], P(None, ('seq', 'fsdp')), may hold values from -3 to 3
- conv_bias: bfloat16 [1536], P(('seq', 'fsdp')), may hold values from -0.5 to 0.5
- state_proj: bfloat16 [1536, 80], P(('seq', 'fsdp')), may hold values from -0.15625 to 0.15625
- step_proj: bfloat16 [48, 1536], P(None, ('seq', 'fsdp')), may hold values from -0.875 to 0.875
- step_bias: bfloat16 [1536], P(('seq', 'fsdp')), may hold values from -6 to -2
- decay_log: bfloat16 [16, 1536], P(None, ('seq', 'fsdp')), may hold values from -9 to 1
- skip_gain: bfloat16 [1536], P(('seq', 'fsdp')), may hold values from 0.5 to 1.5
- out_proj: bfloat16 [1536, 768], P(('seq', 'fsdp')), may hold values from -0.15625 to 0.15625
- norm_gain: bfloat16 [768], P(('seq', 'fsdp')), may hold values from 0.099609375 to 1.8984375
- moe_gain: bfloat16 [768], P(('seq', 'fsdp')), may hold values from 0.099609375 to 1.8984375
- router: bfloat16 [768, 8], P(('seq', 'fsdp')), may hold values from -0.15625 to 0.15625
- expert_up: bfloat16 [8, 768, 3072], P('fsdp', 'seq'), may hold values from -0.21875 to 0.21875
- expert_down: bfloat16 [8, 3072, 768], P('fsdp', 'seq'), may hold values from -0.625 to 0.625
Outputs:
- mixed: bfloat16 [2, 16384, 768], P(None, ('seq', 'fsdp'))
- grad_input: float32 [2, 16384, 768], P(None, ('seq', 'fsdp'))
- grad_in_proj: float32 [768, 3072], P(('seq', 'fsdp'))
- grad_conv_weight: float32 [4, 1536], P(None, ('seq', 'fsdp'))
- grad_conv_bias: float32 [1536], P(('seq', 'fsdp'))
- grad_state_proj: float32 [1536, 80], P(('seq', 'fsdp'))
- grad_step_proj: float32 [48, 1536], P(None, ('seq', 'fsdp'))
- grad_step_bias: float32 [1536], P(('seq', 'fsdp'))
- grad_decay_log: float32 [16, 1536], P(None, ('seq', 'fsdp'))
- grad_skip_gain: float32 [1536], P(('seq', 'fsdp'))
- grad_out_proj: float32 [1536, 768], P(('seq', 'fsdp'))
- grad_norm_gain: float32 [768], P(('seq', 'fsdp'))
- grad_moe_gain: float32 [768], P(('seq', 'fsdp'))
- grad_router: float32 [768, 8], P(('seq', 'fsdp'))
- grad_expert_up: float32 [8, 768, 3072], P('fsdp', 'seq')
- grad_expert_down: float32 [8, 3072, 768], P('fsdp', 'seq')
The draws below stay inside these ranges and needn't reach their ends.
Inputs may be any that keep to these rules, and one draw needn't show every extreme that they name: `routes`: among the 128 rows of one device in one micro-batch (aligned blocks of 128 tokens of a sequence), no expert is named by more than 20 rows, a bound that some block reaches.
All inputs are finite; a program needn't handle non-finite values.
Results may differ from the reference program's by a relative error of at most 0.017.
Values may be sent and summed in bfloat16 or wider, within the bound.
No kernel may reach another device: no remote copies, remote signals or barrier semaphores. Data moves between devices by JAX's collectives and lax.ppermute only.
A program may use at most 768 MiB of HBM per device.

```python
import math
from functools import partial
import jax
import jax.numpy as jnp
import numpy as np
from jax import lax

D = 768
DI = 1536
STATE = 16
RANK = 48
CONV = 4
FF = 3072
TOK_MB = 128
MICRO = 2
EXPERTS = 8
CAP = 20
SEQLEN = 16384


def steps_of(own_key, shape, cuts, low, largest):
    factor_of = 1.0
    for dim, shards_of in cuts:
        heights = jax.random.uniform(jax.random.fold_in(jax.random.fold_in(own_key, 6), dim), (shards_of,), jnp.float32, low / len(cuts), largest / len(cuts))
        factor_of = factor_of * jnp.repeat(jnp.exp(heights), shape[dim] // shards_of).reshape((-1,) + (1,) * (len(shape) - 1 - dim))
    return factor_of


def deal_out(stream_key, own, number, rows, count, top, limit, skew):
    sequence = jax.random.permutation(stream_key, count)
    packed, usual = portions_of(count, rows * top, limit, skew, True), portions_of(count, rows * top, limit, skew, False)
    places = jnp.arange(count)

    def named(sizes, rotation):
        used = int((sizes > 0).sum())
        fixed = max(1, used // 4)
        passed = fixed + (places - fixed + rotation * (used - fixed)) % max(1, count - fixed)
        return jnp.zeros((count,), jnp.int32).at[sequence[jnp.where(places < fixed, places, passed)]].set(jnp.asarray(sizes, jnp.int32))

    sizes = jnp.where(number % 4 == 0, named(packed, number // 4), named(usual, number - number // 4 - 1))
    mixed = jax.random.permutation(jax.random.fold_in(own, 3), count)
    giver, sink = mixed[0:count // 2 * 2:2], mixed[1:count // 2 * 2:2]
    room = jnp.minimum(sizes[giver] - 1, limit - sizes[sink]) // 2
    room = jnp.where((giver == sequence[0]) | (sink == sequence[0]) | (sizes[sink] == 0), 0, jnp.maximum(room, 0))
    passed = jax.random.randint(jax.random.fold_in(own, 4), (count // 2,), 0, 1 << 20) % (room + 1)
    sizes = sizes.at[giver].add(-passed).at[sink].add(passed)
    members = jnp.searchsorted(jnp.cumsum(sizes), jnp.arange(rows * top), side="right").astype(jnp.int32)
    table = members.reshape(top, rows).T
    table = table[jax.random.permutation(jax.random.fold_in(own, 1), rows)]
    rotation = jax.random.randint(jax.random.fold_in(own, 2), (rows, 1), 0, top)
    return jnp.take_along_axis(table, (jnp.arange(top)[None, :] + rotation) % top, axis=1)


def portions_of(count, total, limit, slope, full):
    portions = [(1 << 20) // math.isqrt(rank ** slope) + 1 for rank in range(1, count + 1)]
    largest = limit if full else min(limit, max(-(-total // count), total * portions[0] // sum(portions)))
    least = 1 if total - largest >= count - 1 else 0
    holding, surplus = [largest] + [least] * (count - 1), total - largest - least * (count - 1)
    while surplus > 0:
        free = [i for i in range(1, count) if holding[i] < largest] or [i for i in range(1, count) if holding[i] < limit]
        pool, budget = sum([portions[i] for i in free]), surplus
        for i in free:
            extra = min(limit - holding[i], max(1, budget * portions[i] // pool), surplus)
            holding[i] = holding[i] + extra
            surplus = surplus - extra
    return np.array(holding)


def centred(rng, extent, spread, most, cuts=(), kind=jnp.bfloat16):
    result = spread * jax.random.normal(rng, extent, jnp.float32)
    if cuts:
        result = result * steps_of(rng, extent, cuts, -0.22, 0.18)
    return jnp.clip(result, -most, most).astype(kind)


def setup_inputs(seed: int = 0) -> dict:
    arg_keys = jax.random.split(jax.random.key(seed), 18)
    block_input = centred(arg_keys[0], (MICRO, SEQLEN, D), 1.0, 6.0, ((1, 128),))
    routes_keys = jax.random.split(jax.random.fold_in(arg_keys[1], 1), MICRO * SEQLEN // TOK_MB)
    routes_turns = jax.random.permutation(jax.random.fold_in(arg_keys[1], 3), MICRO * SEQLEN // TOK_MB)
    routes = jax.vmap(lambda own, number: deal_out(jax.random.fold_in(arg_keys[1], 2), own, number, TOK_MB, EXPERTS, 1, CAP, 1))(routes_keys, routes_turns).reshape((MICRO, SEQLEN, 1))
    cotangent = centred(arg_keys[2], (MICRO, SEQLEN, D), 1.0, 6.0, ((1, 128),))
    in_proj = centred(arg_keys[3], (D, 2 * DI), D ** -0.5, 0.21875, ((0, 128),))
    conv_weight = centred(arg_keys[4], (CONV, DI), 0.5, 3.0, ((1, 128),))
    conv_bias = jnp.clip(jax.random.uniform(arg_keys[5], (DI,), jnp.float32, -0.5, 0.5) * steps_of(arg_keys[5], (DI,), ((0, 128),), -0.4, 0.0), -0.5, 0.5).astype(jnp.bfloat16)
    state_proj = centred(arg_keys[6], (DI, RANK + 2 * STATE), DI ** -0.5, 0.15625, ((0, 128),))
    step_proj = centred(arg_keys[7], (RANK, DI), RANK ** -0.5, 0.875, ((1, 128),))
    step_bias = jnp.clip(-6.0 + 4.0 * jax.random.uniform(arg_keys[8], (DI,), jnp.float32) ** steps_of(arg_keys[8], (DI,), ((0, 128),), -0.2, 0.2), -6.0, -2.0).astype(jnp.bfloat16)
    decay_log = jnp.clip(-9.0 + 10.0 * jax.random.uniform(arg_keys[9], (STATE, DI), jnp.float32) ** steps_of(arg_keys[9], (STATE, DI), ((1, 128),), -0.2, 0.2), -9.0, 1.0).astype(jnp.bfloat16)
    skip_gain = jnp.clip(0.5 + 1.0 * jax.random.uniform(arg_keys[10], (DI,), jnp.float32) ** steps_of(arg_keys[10], (DI,), ((0, 128),), -0.2, 0.2), 0.5, 1.5).astype(jnp.bfloat16)
    out_proj = centred(arg_keys[11], (DI, D), DI ** -0.5, 0.15625, ((0, 128),))
    norm_gain = jnp.clip(1.0 + 0.18 * jax.random.normal(arg_keys[12], (D,), jnp.float32), 0.099609375, 1.8984375).astype(jnp.bfloat16)
    moe_gain = jnp.clip(1.0 + 0.18 * jax.random.normal(arg_keys[13], (D,), jnp.float32), 0.099609375, 1.8984375).astype(jnp.bfloat16)
    router = centred(arg_keys[14], (D, EXPERTS), (2 * D) ** -0.5, 0.15625, ((0, 128),))
    expert_up = centred(arg_keys[15], (EXPERTS, D, FF), D ** -0.5, 0.21875, ((0, 8), (1, 16)))
    expert_down = centred(arg_keys[16], (EXPERTS, FF, D), (FF // 36) ** -0.5, 0.625, ((0, 8), (1, 16)))
    return dict(block_input=block_input, routes=routes, cotangent=cotangent, in_proj=in_proj, conv_weight=conv_weight, conv_bias=conv_bias, state_proj=state_proj, step_proj=step_proj, step_bias=step_bias, decay_log=decay_log, skip_gain=skip_gain, out_proj=out_proj, norm_gain=norm_gain, moe_gain=moe_gain, router=router, expert_up=expert_up, expert_down=expert_down)


EPSILON = 1e-05
HIGHEST = lax.Precision.HIGHEST

@jax.custom_vjp
def low(v):
    return lax.optimization_barrier(v.astype(jnp.bfloat16)).astype(jnp.float32)

@jax.custom_vjp
def low_back(v):
    return v

def low_keep(v):
    return (low(v), None)

def low_pass(kept, grad):
    return (grad,)

def back_keep(v):
    return (v, None)

def back_low(kept, grad):
    return (low(grad),)
low.defvjp(low_keep, low_pass)
low_back.defvjp(back_keep, back_low)

def rms_scale(values, scale_gain):
    return values * lax.rsqrt(lax.optimization_barrier(jnp.mean(values * values, axis=-1, keepdims=True)) + EPSILON) * scale_gain

def matmul(first_op, second_op):
    return jnp.dot(first_op, second_op, precision=HIGHEST, preferred_element_type=jnp.float32)

def scan_block(carry, pieces):
    state, decay = carry

    def advance(hidden, column):
        input_row, step_row, in_map, out_map = column
        hidden = jnp.exp(step_row[None, :] * decay) * hidden + in_map[:, None] * (step_row * input_row)[None, :]
        return (hidden, lax.optimization_barrier(jnp.sum(hidden * out_map[:, None], axis=0)))
    state, outputs = lax.scan(advance, state, pieces)
    return ((state, decay), outputs)

def forward(routes_row, block_rows, in_proj, conv_weight, conv_bias, state_proj, step_proj, step_bias, decay_log, skip_gain, out_proj, norm_gain, moe_gain, router, expert_up, expert_down):
    length = block_rows.shape[0]
    blocks = length // TOK_MB
    normed_in = low(rms_scale(block_rows, norm_gain))
    projected = low_back(matmul(normed_in, in_proj))
    conv_input = low(projected[:, :DI])
    gate_branch = projected[:, DI:]
    padded = jnp.concatenate([jnp.zeros((CONV - 1, DI), jnp.float32), conv_input], axis=0)
    conv_sum = conv_bias + conv_weight[0] * padded[0:length]
    for offset in range(1, CONV):
        conv_sum = conv_sum + conv_weight[offset] * padded[offset:offset + length]
    conv_output = low(jax.nn.silu(conv_sum))
    state_inputs = low_back(matmul(conv_output, state_proj))
    step_low = low(state_inputs[:, :RANK])
    input_map = state_inputs[:, RANK:RANK + STATE]
    output_map = state_inputs[:, RANK + STATE:]
    step_size = jax.nn.softplus(low_back(matmul(step_low, step_proj)) + step_bias)
    decay = -jnp.exp(decay_log)
    pieces = (conv_output.reshape(blocks, TOK_MB, DI), step_size.reshape(blocks, TOK_MB, DI), input_map.reshape(blocks, TOK_MB, STATE), output_map.reshape(blocks, TOK_MB, STATE))
    carry = (jnp.zeros((STATE, DI), jnp.float32), decay)
    carry, scan_output = lax.scan(jax.checkpoint(scan_block), carry, pieces)
    scan_output = scan_output.reshape(length, DI)
    gated_output = low((scan_output + skip_gain * conv_output) * jax.nn.silu(gate_branch))
    residual = block_rows + low_back(matmul(gated_output, out_proj))
    normed_moe = low(rms_scale(residual, moe_gain))
    probabilities = jax.nn.softmax(matmul(normed_moe, router), axis=-1)
    chosen = routes_row[:, 0].astype(jnp.int32)
    one_hot = (chosen[:, None] == jnp.arange(EXPERTS, dtype=jnp.int32)[None, :]).astype(jnp.int32)
    expert_gate = lax.optimization_barrier(jnp.sum(probabilities * one_hot.astype(jnp.float32), axis=-1))
    running = jnp.cumsum(one_hot.reshape(blocks, TOK_MB, EXPERTS), axis=1).reshape(length, EXPERTS)
    slot_index = lax.optimization_barrier(jnp.sum((running - 1) * one_hot, axis=-1)).astype(jnp.int32)
    block_index = jnp.arange(length, dtype=jnp.int32) // TOK_MB
    position = (chosen * (blocks * CAP) + block_index * CAP + slot_index).astype(jnp.int32)
    buffer_rows = jnp.zeros((EXPERTS * blocks * CAP, D), jnp.float32).at[position].set(normed_moe)
    buffer_rows = buffer_rows.reshape(EXPERTS, blocks * CAP, D)
    pre_act = low_back(jnp.einsum('erd,edf->erf', buffer_rows, expert_up, precision=HIGHEST))
    hidden = low(jax.nn.gelu(pre_act, approximate=True))
    expert_out = low_back(low(jnp.einsum('erf,efd->erd', hidden, expert_down, precision=HIGHEST)))
    returned = expert_out.reshape(EXPERTS * blocks * CAP, D)[position]
    return residual + expert_gate[:, None] * returned

def reference(block_input, routes, cotangent, in_proj, conv_weight, conv_bias, state_proj, step_proj, step_bias, decay_log, skip_gain, out_proj, norm_gain, moe_gain, router, expert_up, expert_down):
    weights = tuple((array.astype(jnp.float32) for array in (in_proj, conv_weight, conv_bias, state_proj, step_proj, step_bias, decay_log, skip_gain, out_proj, norm_gain, moe_gain, router, expert_up, expert_down)))
    mixed_rows = []
    input_grads = []
    grad_sums = None
    for batch_index in range(MICRO):
        output, pullback = jax.vjp(partial(forward, routes[batch_index]), block_input[batch_index].astype(jnp.float32), *weights)
        grads = pullback(cotangent[batch_index].astype(jnp.float32))
        mixed_rows.append(output.astype(jnp.bfloat16))
        input_grads.append(grads[0])
        if grad_sums is None:
            grad_sums = tuple(grads[1:])
        else:
            grad_sums = tuple((summed + added for summed, added in zip(grad_sums, grads[1:])))
    return (jnp.stack(mixed_rows), jnp.stack(input_grads), grad_sums[0], grad_sums[1], grad_sums[2], grad_sums[3], grad_sums[4], grad_sums[5], grad_sums[6], grad_sums[7], grad_sums[8], grad_sums[9], grad_sums[10], grad_sums[11], grad_sums[12], grad_sums[13])
```

```python
from functools import partial

import jax
import jax.numpy as jnp
from jax import lax
from jax.experimental import pallas as pl
from jax.experimental.pallas import tpu as pltpu
from jax.sharding import PartitionSpec as P

D = 768
DI = 1536
STATE = 16
RANK = 48
CONV = 4
FF = 3072
TOK = 128
MICRO = 2
EXPERTS = 8
DEVICES = 128
WEIGHT_ROWS = 152
CAP = 20
LANES = 128
CB = 384
NCB = DI // CB
TILES = CB // LANES
HEAD = 8
ALL = ("seq", "fsdp")
EPSILON = 1e-05
LOG2E = 1.4426950408889634
LN2 = 0.6931471805599453
MIB = 1024 * 1024
HIGHEST = lax.Precision.HIGHEST
bf16 = jnp.bfloat16
f32 = jnp.float32


def dot(a, b, ca, cb, precision=None):
    return lax.dot_general(
        a, b, (((ca,), (cb,)), ((), ())), precision=precision, preferred_element_type=f32
    )


def silu_parts(v):
    s = jax.nn.sigmoid(v)
    return v * s, s * (1.0 + v * (1.0 - s))


def tile_of(j):
    return slice(j * LANES, (j + 1) * LANES)


def fold_rows(parts):
    row = lax.broadcasted_iota(jnp.int32, (8, LANES), 0)
    parts = [p[:8] + p[8:] for p in parts]
    for d in (1, 2, 4):
        low = (row & d) == 0
        parts = [
            jnp.where(low, a, b) + pltpu.roll(jnp.where(low, b, a), 8 - d, 0)
            for a, b in zip(parts[0::2], parts[1::2])
        ]
    return parts[0]


def load_decay(weights_ref):
    rows = weights_ref[128:144, :].astype(f32)
    return [(-LOG2E) * jnp.exp(rows[:, tile_of(j)]) for j in range(TILES)]


def load_state(ref):
    state = ref[...].reshape(STATE, CB)
    return tuple(state[:, tile_of(j)] for j in range(TILES))


def aligned(tb):
    return pl.ds(pl.multiple_of(tb * 8, 8), 8)


ZERO_STATE = (STATE, LANES)


def end_state_kernel(step_ref, conv_ref, b_ref, weights_ref, out_ref):
    decay = load_decay(weights_ref)

    def block(tb, hs):
        hs = list(hs)
        dt8 = step_ref[0, aligned(tb), :]
        u8 = dt8 * conv_ref[0, aligned(tb), :]
        for i in range(8):
            b = b_ref[0, tb * 8 + i]
            for j in range(TILES):
                dt = dt8[i : i + 1, tile_of(j)]
                u = u8[i : i + 1, tile_of(j)]
                hs[j] = jnp.exp2(dt * decay[j]) * hs[j] + b * u
        return tuple(hs)

    zero = jnp.zeros(ZERO_STATE, f32)
    hs = lax.fori_loop(0, TOK // 8, block, (zero,) * TILES)
    total = jnp.sum(step_ref[0], axis=0, keepdims=True)
    for j in range(TILES):
        prod = jnp.exp2(total[:, tile_of(j)] * decay[j])
        out_ref[:, :, tile_of(j)] = prod.reshape(STATE, 1, LANES)
        out_ref[:, :, tile_of(j + TILES)] = hs[j].reshape(STATE, 1, LANES)


def scan_kernel(
    step_ref, conv_ref, b_ref, c_ref, weights_ref, start_ref, act_ref, my_ref, gated_ref
):
    decay = load_decay(weights_ref)
    skip = weights_ref[144:152, :].astype(f32)[6:7]

    def block(tb, hs):
        hs = list(hs)
        dt8 = step_ref[0, aligned(tb), :]
        conv8 = conv_ref[0, aligned(tb), :]
        u8 = dt8 * conv8
        outs = [[] for _ in range(TILES)]
        for i in range(8):
            t = tb * 8 + i
            b = b_ref[0, t]
            c = c_ref[0, t]
            for j in range(TILES):
                dt = dt8[i : i + 1, tile_of(j)]
                u = u8[i : i + 1, tile_of(j)]
                hs[j] = jnp.exp2(dt * decay[j]) * hs[j] + b * u
                outs[j].append(hs[j] * c)
        for j in range(TILES):
            my_ref[0, aligned(tb), tile_of(j)] = (
                fold_rows(outs[j]) + skip[:, tile_of(j)] * conv8[:, tile_of(j)]
            )
        return tuple(hs)

    lax.fori_loop(0, TOK // 8, block, load_state(start_ref))
    gated_ref[0] = (my_ref[0] * act_ref[0]).astype(bf16)


def history_kernel(step_ref, conv_ref, b_ref, weights_ref, start_ref, ah_ref):
    decay = load_decay(weights_ref)

    def block(tb, hs):
        hs = list(hs)
        dt8 = step_ref[0, aligned(tb), :]
        u8 = dt8 * conv_ref[0, aligned(tb), :]
        for i in range(8):
            t = tb * 8 + i
            b = b_ref[0, t]
            for j in range(TILES):
                dt = dt8[i : i + 1, tile_of(j)]
                u = u8[i : i + 1, tile_of(j)]
                ah = jnp.exp2(dt * decay[j]) * hs[j]
                ah_ref[0, t, :, tile_of(j)] = ah
                hs[j] = ah + b * u
        return tuple(hs)

    lax.fori_loop(0, TOK // 8, block, load_state(start_ref))


def end_adjoint_kernel(step_ref, gy_ref, c_ref, weights_ref, mu_ref):
    decay = load_decay(weights_ref)

    def block(k, mus):
        mus = list(mus)
        tb = TOK // 8 - 1 - k
        dt8 = step_ref[0, aligned(tb), :]
        gy8 = gy_ref[0, aligned(tb), :]
        for i in reversed(range(8)):
            c = c_ref[0, tb * 8 + i]
            for j in range(TILES):
                dt = dt8[i : i + 1, tile_of(j)]
                gy = gy8[i : i + 1, tile_of(j)]
                mus[j] = jnp.exp2(dt * decay[j]) * (mus[j] + c * gy)
        return tuple(mus)

    zero = jnp.zeros(ZERO_STATE, f32)
    mus = lax.fori_loop(0, TOK // 8, block, (zero,) * TILES)
    for j in range(TILES):
        mu_ref[:, :, tile_of(j)] = mus[j].reshape(STATE, 1, LANES)


def scan_back_kernel(
    step_ref,
    sig_ref,
    conv_ref,
    gy_ref,
    ah_ref,
    b_ref,
    c_ref,
    weights_ref,
    later_ref,
    cin_ref,
    low_ref,
    first_ref,
    gcin_ref,
    second_ref,
    glow_ref,
    s1_ref,
    s2_ref,
    gb_ref,
    gc_ref,
):
    phase = pl.program_id(1)

    @pl.when(phase == 0)
    def _():
        gb_ref[...] = jnp.zeros_like(gb_ref)
        gc_ref[...] = jnp.zeros_like(gc_ref)
        glow_ref[...] = jnp.zeros_like(glow_ref)

    @pl.when(phase < NCB)
    def _():
        decay = load_decay(weights_ref)

        def backward(k, carry):
            mus, gds = list(carry[0]), list(carry[1])
            tb = TOK // 8 - 1 - k
            dt8 = step_ref[0, aligned(tb), :]
            u8 = dt8 * conv_ref[0, aligned(tb), :]
            gy8 = gy_ref[0, aligned(tb), :]
            out1 = [[None] * 8 for _ in range(TILES)]
            out2 = [[None] * 8 for _ in range(TILES)]
            for i in reversed(range(8)):
                t = tb * 8 + i
                b = b_ref[0, t]
                c = c_ref[0, t]
                gb = gb_ref[t]
                gc = gc_ref[t]
                for j in range(TILES):
                    dt = dt8[i : i + 1, tile_of(j)]
                    u = u8[i : i + 1, tile_of(j)]
                    gy = gy8[i : i + 1, tile_of(j)]
                    ah = ah_ref[0, t, :, tile_of(j)]
                    lam = c * gy + mus[j]
                    w = lam * ah * decay[j]
                    out1[j][i] = lam * b
                    out2[j][i] = w
                    gds[j] = gds[j] + w * dt
                    gb = gb + lam * u
                    gc = gc + gy * (ah + b * u)
                    mus[j] = jnp.exp2(dt * decay[j]) * lam
                gb_ref[t] = gb
                gc_ref[t] = gc
            for j in range(TILES):
                s1_ref[phase, aligned(tb), tile_of(j)] = fold_rows(out1[j])
                s2_ref[aligned(tb), tile_of(j)] = fold_rows(out2[j])
            return tuple(mus), tuple(gds)

        zero = jnp.zeros(ZERO_STATE, f32)
        _, gds = lax.fori_loop(
            0, TOK // 8, backward, (load_state(later_ref), (zero,) * TILES)
        )
        for j in range(TILES):
            first_ref[0, 48:64, tile_of(j)] = LN2 * gds[j]
        gsp = (LN2 * s2_ref[...] + conv_ref[0] * s1_ref[phase]) * sig_ref[0]
        gsp_low = gsp.astype(bf16)
        first_ref[0, 0:48, :] = dot(low_ref[0], gsp_low, 0, 0)
        first_ref[0, 64:72, :] = jnp.broadcast_to(
            jnp.sum(gsp, axis=0, keepdims=True), (8, CB)
        )
        glow_ref[:, 0:48] += dot(gsp_low, weights_ref[80:128, :], 1, 1)

    @pl.when(phase == NCB)
    def _():
        glow_ref[:, 48:64] = jnp.sum(gb_ref[...], axis=-1)
        glow_ref[:, 64:80] = jnp.sum(gc_ref[...], axis=-1)

    @pl.when(phase >= NCB)
    def _():
        gy = gy_ref[0]
        conv = conv_ref[0]
        vecs = weights_ref[144:152, :].astype(f32)
        glow = glow_ref[...].astype(bf16)
        gconv = (
            step_ref[0] * s1_ref[phase - NCB]
            + vecs[6:7] * gy
            + dot(glow, weights_ref[0:80, :], 1, 0)
        )
        second_ref[0, 0:80, :] = dot(glow, conv.astype(bf16), 0, 0)
        cin = cin_ref[0].astype(f32)
        first = HEAD - CONV + 1
        pieces = [cin[first + i : first + i + TOK] for i in range(CONV)]
        v = vecs[4:5] + sum(vecs[i : i + 1] * pieces[i] for i in range(CONV))
        gv = gconv * silu_parts(v)[1]
        for i in range(CONV):
            second_ref[0, 80 + i : 81 + i, :] = jnp.sum(gv * pieces[i], axis=0, keepdims=True)
        second_ref[0, 84:85, :] = jnp.sum(gv, axis=0, keepdims=True)
        second_ref[0, 85:86, :] = jnp.sum(gy * conv, axis=0, keepdims=True)
        second_ref[0, 86:88, :] = jnp.zeros((2, CB), f32)
        edge = jnp.zeros((8, CB), f32)
        padded = jnp.concatenate([edge, gv, edge], axis=0)
        gcin_ref[0] = sum(
            vecs[i : i + 1] * padded[CONV - 1 - i : CONV - 1 - i + TOK + HEAD]
            for i in range(CONV)
        )


def same(c):
    return c


def at(c):
    return jnp.minimum(c, NCB - 1)


def wrap(c):
    return lax.rem(c, NCB)


def second(c):
    return jnp.maximum(c - NCB, 0)


def token_spec(place=same, rows=TOK):
    return pl.BlockSpec((1, rows, CB), lambda m, c: (m, 0, place(c)))


def weights_spec(place=same):
    return pl.BlockSpec((WEIGHT_ROWS, CB), lambda m, c: (0, place(c)))


MAP_SPEC = pl.BlockSpec((1, TOK, STATE, LANES), lambda m, c: (m, 0, 0, 0))


def state_spec(width=CB, place=same):
    return pl.BlockSpec((STATE, 1, width), lambda m, c: (m * NCB + place(c), 0, 0))


def history_spec(place=same):
    return pl.BlockSpec((1, TOK, STATE, CB), lambda m, c: (m, 0, 0, place(c)))


def shape_of(*shape, dtype=f32):
    return jax.ShapeDtypeStruct(shape, dtype)


PARAMS = pltpu.CompilerParams(
    dimension_semantics=("arbitrary", "arbitrary"), vmem_limit_bytes=48 * MIB
)


def lasting(us):
    return pl.CostEstimate(flops=us * 10**9, bytes_accessed=us * 3 * 10**6, transcendentals=0)


def end_state(step, conv, in_map, weights):
    return pl.pallas_call(
        end_state_kernel,
        grid=(MICRO, NCB),
        in_specs=[token_spec(), token_spec(), MAP_SPEC, weights_spec()],
        out_specs=state_spec(2 * CB),
        out_shape=shape_of(DEVICES, 1, 2 * CB),
        compiler_params=PARAMS,
        cost_estimate=lasting(6),
        name="end_state",
    )(step, conv, in_map, weights)


def scan(step, conv, in_map, out_map, weights, start, act):
    return pl.pallas_call(
        scan_kernel,
        grid=(MICRO, NCB),
        in_specs=[
            token_spec(),
            token_spec(),
            MAP_SPEC,
            MAP_SPEC,
            weights_spec(),
            state_spec(),
            token_spec(),
        ],
        out_specs=[token_spec(), token_spec()],
        out_shape=[shape_of(MICRO, TOK, DI), shape_of(MICRO, TOK, DI, dtype=bf16)],
        compiler_params=PARAMS,
        cost_estimate=lasting(12),
        name="scan",
    )(step, conv, in_map, out_map, weights, start, act)


def history(step, conv, in_map, weights, start):
    return pl.pallas_call(
        history_kernel,
        grid=(MICRO, NCB),
        in_specs=[token_spec(), token_spec(), MAP_SPEC, weights_spec(), state_spec()],
        out_specs=history_spec(),
        out_shape=shape_of(MICRO, TOK, STATE, DI),
        compiler_params=PARAMS,
        cost_estimate=lasting(12),
        name="history",
    )(step, conv, in_map, weights, start)


def end_adjoint(step, gy, out_map, weights):
    return pl.pallas_call(
        end_adjoint_kernel,
        grid=(MICRO, NCB),
        in_specs=[token_spec(), token_spec(), MAP_SPEC, weights_spec()],
        out_specs=state_spec(),
        out_shape=shape_of(DEVICES, 1, CB),
        compiler_params=PARAMS,
        cost_estimate=lasting(6),
        name="end_adjoint",
    )(step, gy, out_map, weights)


def scan_back(step, sig, conv, gy, ah, in_map, out_map, weights, later, cin, low):
    return pl.pallas_call(
        scan_back_kernel,
        grid=(MICRO, 2 * NCB),
        in_specs=[
            token_spec(wrap),
            token_spec(at),
            token_spec(wrap),
            token_spec(wrap),
            history_spec(at),
            MAP_SPEC,
            MAP_SPEC,
            weights_spec(wrap),
            state_spec(CB, at),
            token_spec(second, TOK + HEAD),
            pl.BlockSpec((1, TOK, RANK), lambda m, c: (m, 0, 0)),
        ],
        out_specs=[
            token_spec(at, 72),
            token_spec(second, TOK + HEAD),
            token_spec(second, 88),
        ],
        out_shape=[
            shape_of(MICRO, 72, DI),
            shape_of(MICRO, TOK + HEAD, DI),
            shape_of(MICRO, 88, DI),
        ],
        scratch_shapes=[
            pltpu.VMEM((TOK, 80), f32),
            pltpu.VMEM((NCB, TOK, CB), f32),
            pltpu.VMEM((TOK, CB), f32),
            pltpu.VMEM((TOK, STATE, LANES), f32),
            pltpu.VMEM((TOK, STATE, LANES), f32),
        ],
        compiler_params=PARAMS,
        cost_estimate=lasting(36),
        name="scan_back",
    )(step, sig, conv, gy, ah, in_map, out_map, weights, later, cin, low)


def prefix_kernel(reverse, prod_ref, state_ref, out_ref):
    skipped = state_ref.shape[2] - CB

    def one(k, state):
        i = DEVICES - 1 - k if reverse else k
        out_ref[i] = state
        return prod_ref[i, :, :CB] * state + state_ref[i, :, skipped:]

    lax.fori_loop(0, DEVICES, one, jnp.zeros((1, CB), f32), unroll=8)


def prefix(prod, state, reverse):
    return pl.pallas_call(
        partial(prefix_kernel, reverse),
        out_shape=shape_of(DEVICES, 1, CB),
        cost_estimate=lasting(2),
        name="prefix",
    )(prod, state)


ROWS = EXPERTS * MICRO * CAP
FB = 768
NFB = FF // FB
EXP_PARAMS = pltpu.CompilerParams(
    dimension_semantics=("arbitrary",), vmem_limit_bytes=56 * MIB
)


def gelu_parts(v):
    c = 0.7978845608028654
    v2 = v * v
    th = jnp.tanh(c * (v + 0.044715 * v * v2))
    half = 0.5 * (1.0 + th)
    return v * half, half + 0.5 * v * (1.0 - th * th) * c * (1.0 + 3 * 0.044715 * v2)


def expert_kernel(rows_ref, up_ref, down_ref, hidden_ref, gpre_ref, out_ref, acc_ref):
    j = pl.program_id(0)
    up = up_ref[...].reshape(D, FB)
    down = down_ref[...].reshape(FB, D)
    x = rows_ref[:, :D]
    g = rows_ref[:, D:]
    act, slope = gelu_parts(dot(x, up, 1, 0))
    hidden = act.astype(bf16)
    gpre = (dot(g, down, 1, 1) * slope).astype(bf16)
    hidden_ref[...] = hidden
    gpre_ref[...] = gpre
    eo = dot(hidden, down, 1, 0)
    gr = dot(gpre, up, 1, 1)

    @pl.when(j == 0)
    def _():
        acc_ref[:, :D] = eo
        acc_ref[:, D:] = gr

    @pl.when(j > 0)
    def _():
        acc_ref[:, :D] += eo
        acc_ref[:, D:] += gr

    @pl.when(j == NFB - 1)
    def _():
        out_ref[...] = acc_ref[...].astype(bf16)


def expert_call(rows, weights):
    return pl.pallas_call(
        expert_kernel,
        grid=(NFB,),
        in_specs=[
            pl.BlockSpec((ROWS, 2 * D), lambda j: (0, 0)),
            pl.BlockSpec((16, 48, D), lambda j: (0, j, 0)),
            pl.BlockSpec((4, 192, D), lambda j: (j, 1, 0)),
        ],
        out_specs=[
            pl.BlockSpec((ROWS, FB), lambda j: (0, j)),
            pl.BlockSpec((ROWS, FB), lambda j: (0, j)),
            pl.BlockSpec((ROWS, 2 * D), lambda j: (0, 0)),
        ],
        out_shape=[
            jax.ShapeDtypeStruct((ROWS, FF), bf16),
            jax.ShapeDtypeStruct((ROWS, FF), bf16),
            jax.ShapeDtypeStruct((ROWS, 2 * D), bf16),
        ],
        scratch_shapes=[pltpu.VMEM((ROWS, 2 * D), f32)],
        compiler_params=EXP_PARAMS,
        cost_estimate=lasting(11),
        name="expert",
    )(rows, weights, weights)


def expert_grad_kernel(rows_ref, hidden_ref, gpre_ref, out_ref):
    j = pl.program_id(0)
    gup = dot(rows_ref[:, :D], gpre_ref[...], 0, 0).astype(bf16)
    gdown = dot(hidden_ref[...], rows_ref[:, D:], 0, 0).astype(bf16)
    out_ref[:, pl.ds(pl.multiple_of(j * 48, 16), 48), :] = gup.reshape(16, 48, D)
    out_ref[pl.ds(j * 4, 4), 192:384, :] = gdown.reshape(4, 192, D)


def expert_grad_call(rows, hidden, gpre):
    return pl.pallas_call(
        expert_grad_kernel,
        grid=(NFB,),
        in_specs=[
            pl.BlockSpec((ROWS, 2 * D), lambda j: (0, 0)),
            pl.BlockSpec((ROWS, FB), lambda j: (0, j)),
            pl.BlockSpec((ROWS, FB), lambda j: (0, j)),
        ],
        out_specs=pl.BlockSpec((16, 384, D), lambda j: (0, 0, 0)),
        out_shape=shape_of(16, 576, D, dtype=bf16),
        compiler_params=EXP_PARAMS,
        cost_estimate=lasting(11),
        name="expert_grad",
    )(rows, hidden, gpre)


def picks(natural, size):
    shape = (size, natural.shape[1])
    return (lax.broadcasted_iota(jnp.int32, shape, 0) == natural).astype(bf16)


def split_dot(a, b):
    high = a.astype(bf16)
    low = (a - high.astype(f32)).astype(bf16)
    return dot(high, b, 1, 1) + dot(low, b, 1, 1)


def early_grad_kernel(held_ref, gated_ref, mix_ref, normed_ref, branch_ref, out_ref):
    out_ref[:, 0:96, :] = dot(gated_ref[...], mix_ref[...], 0, 0).astype(bf16).reshape(16, 96, D)
    for h in range(2):
        part = dot(normed_ref[...], branch_ref[:, h * D : (h + 1) * D], 0, 0)
        out_ref[:, 96 + 48 * h : 144 + 48 * h, :] = part.astype(bf16).reshape(16, 48, D)


def early_grad_call(held, gated, mix, normed, branch):
    return pl.pallas_call(
        early_grad_kernel,
        grid=(1,),
        in_specs=[
            pl.BlockSpec(memory_space=pl.ANY),
            pl.BlockSpec((MICRO * TOK, DI), lambda j: (0, 0)),
            pl.BlockSpec((MICRO * TOK, D), lambda j: (0, 0)),
            pl.BlockSpec((MICRO * TOK, D), lambda j: (0, 0)),
            pl.BlockSpec((MICRO * TOK, DI), lambda j: (0, 0)),
        ],
        out_specs=pl.BlockSpec((16, 192, D), lambda j: (0, 2, 0)),
        out_shape=shape_of(16, 576, D, dtype=bf16),
        input_output_aliases={0: 0},
        compiler_params=EXP_PARAMS,
        cost_estimate=lasting(12),
        name="early_grad",
    )(held, gated, mix, normed, branch)


def gathered_row(k, rows):
    return (k % (16 * rows) // rows * 8 + k // (16 * rows)) * rows + k % rows


def gate_kernel(normed_ref, late_ref, act_ref, slope_ref, out_ref, total_ref):
    j = pl.program_id(0)
    act, slope = silu_parts(dot(normed_ref[...], late_ref[:, :D], 1, 0))
    act_ref[...] = act
    slope_ref[...] = slope
    k = lax.broadcasted_iota(jnp.int32, (1, D), 1)
    source = (k % 96 // 6 * 8 + k // 96) * 12 + j * 6 + k % 6
    part = dot(picks(source, DI), late_ref[:, D:], 1, 0)

    @pl.when(j == 0)
    def _():
        total_ref[...] = part

    @pl.when(j == 1)
    def _():
        out_ref[...] = (total_ref[...] + part).astype(bf16)


def gate_call(normed, late):
    return pl.pallas_call(
        gate_kernel,
        grid=(2,),
        in_specs=[
            pl.BlockSpec((MICRO * TOK, D), lambda j: (0, 0)),
            pl.BlockSpec((D, DI), lambda j: (0, j)),
        ],
        out_specs=[
            pl.BlockSpec((MICRO * TOK, D), lambda j: (0, j)),
            pl.BlockSpec((MICRO * TOK, D), lambda j: (0, j)),
            pl.BlockSpec((DI, D), lambda j: (0, 0)),
        ],
        out_shape=[
            shape_of(MICRO * TOK, DI),
            shape_of(MICRO * TOK, DI),
            shape_of(DI, D, dtype=bf16),
        ],
        scratch_shapes=[pltpu.VMEM((DI, D), f32)],
        compiler_params=EXP_PARAMS,
        cost_estimate=lasting(12),
        name="gate",
    )(normed, late)


def input_grad_kernel(
    cin_ref,
    branch_ref,
    in_c_ref,
    late_ref,
    x_ref,
    gain_ref,
    residual_ref,
    big_ref,
    out_ref,
    up_ref,
    down_ref,
    rest_ref,
):
    k = lax.broadcasted_iota(jnp.int32, (1, D), 1)
    order = picks(gathered_row(k, 6), D)
    grad = dot(cin_ref[...], in_c_ref[...], 1, 1)
    for h in range(2):
        grad += dot(
            branch_ref[:, h * D : (h + 1) * D], late_ref[:, 2 * h * D : (2 * h + 1) * D], 1, 1
        )
    scaled = split_dot(grad, order) * gain_ref[...]
    x = x_ref[...]
    scale = lax.rsqrt(jnp.mean(x * x, axis=-1, keepdims=True) + EPSILON)
    unit = x * scale
    out_ref[...] = residual_ref[...] + scale * (
        scaled - unit * jnp.mean(scaled * unit, axis=-1, keepdims=True)
    )
    for j in range(NFB):
        up_ref[:, j * FB : (j + 1) * FB] = big_ref[j * 48 : (j + 1) * 48, :].astype(f32)
    down_ref[...] = big_ref[192:384, :].astype(f32)
    rest_ref[...] = big_ref[384:576, :]


def input_grad_call(*args):
    return pl.pallas_call(
        input_grad_kernel,
        out_shape=[
            shape_of(MICRO * TOK, D),
            shape_of(48, FF),
            shape_of(192, D),
            shape_of(192, D, dtype=bf16),
        ],
        compiler_params=pltpu.CompilerParams(vmem_limit_bytes=56 * MIB),
        cost_estimate=lasting(20),
        name="input_grad",
    )(*args)


def swap(v, axis):
    return lax.all_to_all(v, axis, 0, 0, tiled=True)


def spread(v, axis):
    n = lax.axis_size(axis) if isinstance(axis, str) else 128
    return swap(jnp.broadcast_to(v[None], (n,) + v.shape), axis)


def after(done, *values):
    held = lax.optimization_barrier((done,) + values)[1:]
    return held if len(held) > 1 else held[0]


CHIPS = 4
CORE_SWAP = [(i, i ^ 1) for i in range(8)]
HOPS = (1, -1, 2)


def along_z(v, by):
    return lax.ppermute(
        v, "fsdp", [(2 * z + c, 2 * ((z + by) % CHIPS) + c) for z in range(CHIPS) for c in range(2)]
    )


def cores_total(own, other):
    return (own + lax.ppermute(other, "fsdp", CORE_SWAP).astype(f32)).astype(bf16)


def chips_total(parts):
    parts = parts.reshape(CHIPS, parts.shape[0] // CHIPS, parts.shape[1])
    parts = [parts[0]] + [along_z(parts[i + 1], -by) for i, by in enumerate(HOPS)]
    return sum(p.astype(f32) for p in parts).astype(bf16)


def device_of(piece):
    place = lax.axis_index("fsdp")
    chip, core = place // 2, place % 2
    hop = piece % CHIPS
    chip = (chip + jnp.where(hop == 1, 3, jnp.where(hop == 2, 1, hop - hop // 3))) % CHIPS
    return 2 * chip + jnp.where(piece < CHIPS, core, 1 - core)


def on_device(
    block_input,
    routes,
    cotangent,
    in_proj,
    conv_weight,
    conv_bias,
    state_proj,
    step_proj,
    step_bias,
    decay_log,
    skip_gain,
    out_proj,
    norm_gain,
    moe_gain,
    router,
    expert_up,
    expert_down,
):
    T = TOK
    half = D // 2
    small = jnp.concatenate(
        [
            state_proj,
            step_proj.T,
            decay_log.T,
            conv_weight.T,
            conv_bias[:, None],
            step_bias[:, None],
            skip_gain[:, None],
            jnp.zeros((12, 1), bf16),
        ],
        axis=1,
    ).reshape(1, 12 * WEIGHT_ROWS)
    wide = jnp.concatenate([norm_gain[:, None], moe_gain[:, None], router], axis=1)
    packed = jnp.concatenate([small, wide.reshape(1, 60), jnp.zeros((1, 164), bf16)], axis=1)
    rows_c = jnp.concatenate([in_proj[:, :DI].reshape(72, 128), packed.reshape(16, 128)], axis=0)
    rows_c = spread(rows_c, "seq")
    in_c = lax.all_gather(rows_c[:, :72].reshape(96, DI), "fsdp", axis=0, tiled=True)
    packed = lax.all_gather(rows_c[:, 72:].reshape(256, 128), "fsdp", axis=0, tiled=False)
    packed = packed.reshape(8, 16, 2048).transpose(1, 0, 2).reshape(DEVICES, 2048)
    rows_late = jnp.concatenate(
        [in_proj[:, DI : DI + D], out_proj[:6], in_proj[:, DI + D :], out_proj[6:]], axis=1
    )
    rows_late = after(rows_c, rows_late)
    rows_late = spread(rows_late, "seq").reshape(96, 2 * DI)
    late = lax.all_gather(rows_late, "fsdp", axis=0, tiled=True)
    up_rows = expert_up[0].reshape(48, NFB, FB).transpose(1, 0, 2).reshape(192, FB)
    big = jnp.concatenate([up_rows, expert_down[0]], axis=0)

    weights = packed[:, : 12 * WEIGHT_ROWS].reshape(DI, WEIGHT_ROWS).T
    state_w, step_w = weights[:80], weights[80:128]
    vecs = weights[144:152].astype(f32)
    conv_w, conv_b, step_b = vecs[:4], vecs[4:5], vecs[5:6]
    wide = packed[:, 12 * WEIGHT_ROWS : 12 * WEIGHT_ROWS + 60].reshape(D, 10).T
    norm_g, moe_g, router_w = wide[0:1].astype(f32), wide[1:2].astype(f32), wide[2:]

    k = lax.broadcasted_iota(jnp.int32, (1, D), 1)
    order = picks(gathered_row(k, 6), D)

    x_tail = lax.ppermute(block_input[:, T - CONV + 1 :], ALL, [(i, i + 1) for i in range(127)])
    x_head = jnp.concatenate(
        [jnp.zeros((MICRO, HEAD - CONV + 1, D), bf16), x_tail, block_input], axis=1
    ).astype(f32)
    x = x_head[:, HEAD:].reshape(MICRO * T, D)
    x_rows = x_head.reshape(MICRO * (T + HEAD), D)
    scale_head = lax.rsqrt(jnp.mean(x_rows * x_rows, axis=-1, keepdims=True) + EPSILON)
    normed_head = (x_rows * scale_head * norm_g).astype(bf16)
    normed_nat = normed_head.reshape(MICRO, T + HEAD, D)[:, HEAD:].reshape(MICRO * T, D)
    normed_head = dot(normed_head, order, 1, 0).astype(bf16)
    conv_low_in = dot(normed_head, in_c, 1, 0).astype(bf16)
    normed_in = normed_head.reshape(MICRO, T + HEAD, D)[:, HEAD:].reshape(MICRO * T, D)
    conv_low_in = conv_low_in.reshape(MICRO, T + HEAD, DI)
    big = after(conv_low_in, big)
    big = lax.all_gather(big, "seq", axis=0, tiled=False)
    conv_in = conv_low_in.astype(f32)
    first = HEAD - CONV + 1
    v = conv_b + sum(conv_w[i] * conv_in[:, first + i : first + i + T] for i in range(CONV))
    conv_low = jax.nn.silu(v).astype(bf16)
    conv = conv_low.astype(f32)
    conv_low = conv_low.reshape(MICRO * T, DI)
    state_in = dot(conv_low, state_w, 1, 1)
    step_low = state_in[:, :RANK].astype(bf16)
    step_pre = (dot(step_low, step_w, 1, 0) + step_b).reshape(MICRO, T, DI)
    step = jax.nn.softplus(step_pre)
    sig = jax.nn.sigmoid(step_pre)
    in_map = jnp.broadcast_to(
        state_in[:, RANK : RANK + STATE].reshape(MICRO, T, STATE, 1), (MICRO, T, STATE, LANES)
    )
    ends = end_state(step, conv, in_map, weights)
    held_in, normed_in = after(ends, state_in, normed_in)
    pair = swap(ends, ALL)
    gate_act, gate_slope, out_w = gate_call(normed_in, late)
    pair = after(out_w, pair)
    gate_act = gate_act.reshape(MICRO, T, DI)
    gate_slope = gate_slope.reshape(MICRO, T, DI)
    out_map = jnp.broadcast_to(
        held_in[:, RANK + STATE :].reshape(MICRO, T, STATE, 1), (MICRO, T, STATE, LANES)
    )
    start = swap(prefix(pair, pair, False), ALL)
    one_hot_i = (
        routes.reshape(MICRO, T, 1) == lax.broadcasted_iota(jnp.int32, (MICRO, T, EXPERTS), 2)
    ).astype(jnp.int32)
    slot = jnp.sum((jnp.cumsum(one_hot_i, axis=1) - 1) * one_hot_i, axis=2)
    micro = lax.broadcasted_iota(jnp.int32, (MICRO, T), 0)
    position = (routes.reshape(MICRO, T) * (MICRO * CAP) + micro * CAP + slot).reshape(
        1, MICRO * T
    )
    table = (lax.broadcasted_iota(jnp.int32, (ROWS, MICRO * T), 0) == position).astype(bf16)
    one_hot = one_hot_i.reshape(MICRO * T, EXPERTS).astype(f32)
    grad_out = cotangent.reshape(MICRO * T, D).astype(f32)

    mixed_y, gated = scan(step, conv, in_map, out_map, weights, start, gate_act)
    gated = gated.reshape(MICRO * T, DI)
    residual = x + dot(gated, out_w, 1, 0)
    scale_moe = lax.rsqrt(jnp.mean(residual * residual, axis=-1, keepdims=True) + EPSILON)
    normed_moe = (residual * scale_moe * moe_g).astype(bf16)
    probs = jax.nn.softmax(dot(normed_moe, router_w, 1, 1), axis=-1)
    expert_gate = jnp.sum(probs * one_hot, axis=-1, keepdims=True)
    grad_eo = (expert_gate * grad_out).astype(bf16)

    sent = dot(table, jnp.concatenate([normed_moe, grad_eo], axis=1), 1, 0).astype(bf16)
    held_step = after(sent, step)
    sent = swap(sent, "fsdp")
    ah = history(held_step, conv, in_map, weights, start)
    sent = after(ah, sent)
    hidden, grad_pre, back = expert_call(sent, big)
    back = swap(back, "fsdp")
    grad_experts = expert_grad_call(sent, hidden, grad_pre)
    back = after(grad_experts, back)
    returned = dot(table, back, 0, 0)
    expert_out, grad_moe_in = returned[:, :D], returned[:, D:]
    mixed = (residual + expert_gate * expert_out).astype(bf16)

    grad_gate = jnp.sum(grad_out * expert_out, axis=-1, keepdims=True)
    grad_logits = grad_gate * expert_gate * (one_hot - probs)
    grad_moe_in = grad_moe_in + dot(grad_logits, router_w.astype(f32), 1, 0, HIGHEST)
    unit = residual * scale_moe
    scaled = grad_moe_in * moe_g
    grad_residual = grad_out + scale_moe * (
        scaled - unit * jnp.mean(scaled * unit, axis=-1, keepdims=True)
    )
    grad_mix = grad_residual.astype(bf16)
    grad_gated = dot(grad_mix, out_w, 1, 1).reshape(MICRO, T, DI)
    grad_y = grad_gated * gate_act
    grad_gate_branch = (grad_gated * mixed_y * gate_slope).astype(bf16).reshape(MICRO * T, DI)
    mu = end_adjoint(step, grad_y, out_map, weights)
    held_branch, held_gated, held_mix = after(mu, grad_gate_branch, gated, grad_mix)
    mus = swap(mu, ALL)
    grad_big = early_grad_call(grad_experts, held_gated, held_mix, normed_nat, held_branch)
    mus = after(grad_big, mus)
    grad_big = lax.psum_scatter(
        grad_big.reshape(16 * 576, D), "seq", scatter_dimension=0, tiled=True
    )
    later = swap(prefix(pair, mus, True), ALL)
    grad_router = dot(grad_logits, normed_moe.astype(f32), 0, 0, HIGHEST)
    grad_moe_gain = jnp.sum(grad_moe_in * unit, axis=0, keepdims=True)
    wide = jnp.concatenate([grad_moe_gain, grad_router, jnp.zeros((7, D), f32)], axis=0)
    wide = wide.astype(bf16).T.reshape(DEVICES, 1, 96)

    grad_first, grad_cin, grad_second = scan_back(
        step,
        sig,
        conv,
        grad_y,
        ah,
        in_map,
        out_map,
        weights,
        later,
        conv_low_in,
        step_low.reshape(MICRO, T, RANK),
    )
    grad_next = lax.ppermute(grad_cin[:, first:HEAD], ALL, [(i + 1, i) for i in range(127)])
    grad_cin = grad_cin[:, HEAD:] + jnp.pad(grad_next, ((0, 0), (T - CONV + 1, 0), (0, 0)))
    grad_cin = grad_cin.astype(bf16).reshape(MICRO * T, DI)
    smalls = jnp.concatenate(
        [grad_first[0] + grad_first[1], grad_second[0] + grad_second[1]], axis=0
    ).astype(bf16)
    smalls = smalls.T.reshape(DEVICES, 2, 960)
    wide = jnp.pad(wide, ((0, 0), (0, 1), (0, 480)))
    smalls = jnp.concatenate([smalls, wide], axis=2).reshape(DEVICES // 2, 2, 2, DI)

    def for_core(core):
        k = lax.broadcasted_iota(jnp.int32, (1, 512), 1)
        row = k % 8
        inner = picks(jnp.where(row < 6, (k // 8 * 2 + core) * 6 + row, -1), D)
        inner = dot(normed_nat, inner, 1, 0).astype(bf16)
        outer = picks(jnp.where(row < 6, -1, k // 8 * 2 + row - 6), DEVICES)
        more = jnp.where(core == 0, smalls[:, 0], smalls[:, 1]).reshape(DEVICES, DI)
        return dot(inner, grad_cin, 0, 0) + dot(outer, more, 0, 0)

    core = lax.axis_index("fsdp") % 2
    total = cores_total(for_core(core), for_core(1 - core).astype(bf16))
    held_cin, grad_big = after(total, grad_cin, grad_big)
    total = lax.all_to_all(
        total.reshape(64, 8, DI),
        ALL,
        0,
        0,
        tiled=True,
        axis_index_groups=[list(range(c, DEVICES, 2)) for c in (0, 1)],
    )
    grad_input, grad_up, grad_down, rest = input_grad_call(
        held_cin, grad_gate_branch, in_c, late, x, norm_g, grad_residual, grad_big
    )
    k = lax.broadcasted_iota(jnp.int32, (1, 192), 1)
    owner, row = device_of(k // 24), k % 24
    source = jnp.where(row < 12, owner * 12 + row, 96 + row // 18 * 48 + owner * 6 + row % 6)
    rest = dot(picks(source, 192), rest, 0, 0)
    rest = chips_total(cores_total(rest[:96], rest[96:].astype(bf16))).astype(f32)
    total = after(grad_input, total)
    total = jnp.sum(total.astype(f32), axis=0)
    grad_in = jnp.concatenate([total[:6], rest[12:18], rest[18:24]], axis=1)
    grad_norm_gain = jnp.sum(in_proj.astype(f32) * grad_in, axis=1) / norm_gain.astype(f32)
    rows = total[6:, :960].reshape(12, 160)
    rest_rows = rows.T
    wide = total[6, 960:1056].reshape(6, 16)
    return (
        mixed.reshape(MICRO, T, D),
        grad_input.reshape(MICRO, T, D),
        grad_in,
        rest_rows[152:156],
        rest_rows[156],
        rows[:, 72:152],
        rest_rows[:48],
        rest_rows[64],
        rest_rows[48:64],
        rest_rows[157],
        rest[:12],
        grad_norm_gain,
        wide[:, 0],
        wide[:, 1:9],
        grad_up[None],
        grad_down[None],
    )


def solution(mesh):
    return jax.shard_map(
        on_device,
        mesh=mesh,
        in_specs=(
            P(None, ALL, None),
            P(None, ALL, None),
            P(None, ALL, None),
            P(ALL, None),
            P(None, ALL),
            P(ALL),
            P(ALL, None),
            P(None, ALL),
            P(ALL),
            P(None, ALL),
            P(ALL),
            P(ALL, None),
            P(ALL),
            P(ALL),
            P(ALL, None),
            P("fsdp", "seq", None),
            P("fsdp", "seq", None),
        ),
        out_specs=(
            P(None, ALL, None),
            P(None, ALL, None),
            P(ALL, None),
            P(None, ALL),
            P(ALL),
            P(ALL, None),
            P(None, ALL),
            P(ALL),
            P(None, ALL),
            P(ALL),
            P(ALL, None),
            P(ALL),
            P(ALL),
            P(ALL, None),
            P("fsdp", "seq", None),
            P("fsdp", "seq", None),
        ),
        check_vma=False,
    )
```

```python
from functools import partial

import jax
import jax.numpy as jnp
from jax import lax
from jax.experimental import pallas as pl
from jax.experimental.pallas import tpu as pltpu
from jax.sharding import PartitionSpec as P

D = 768
DI = 1536
STATE = 16
RANK = 48
CONV = 4
FF = 3072
TOK = 128
MICRO = 2
EXPERTS = 8
DEVICES = 128
CHIPS = 4
WEIGHT_ROWS = 152
CAP = 20
LANES = 128
CB = 384
NCB = DI // CB
TILES = CB // LANES
HEAD = 8
ALL = ("seq", "fsdp")
EPSILON = 1e-05
LOG2E = 1.4426950408889634
LN2 = 0.6931471805599453
MIB = 1024 * 1024
HIGHEST = lax.Precision.HIGHEST
bf16 = jnp.bfloat16
f32 = jnp.float32


def dot(a, b, ca, cb, precision=None):
    return lax.dot_general(
        a, b, (((ca,), (cb,)), ((), ())), precision=precision, preferred_element_type=f32
    )


def silu_parts(v):
    s = jax.nn.sigmoid(v)
    return v * s, s * (1.0 + v * (1.0 - s))


def tile_of(j):
    return slice(j * LANES, (j + 1) * LANES)


class Fold:
    def __init__(self, falling=False):
        self.held = []
        self.falling = falling

    def add(self, part):
        part, level = part[:8] + part[8:], 0
        while self.held and self.held[-1][1] == level:
            other = self.held.pop()[0]
            a, b = (part, other) if self.falling else (other, part)
            d = 1 << level
            low = (lax.broadcasted_iota(jnp.int32, (8, LANES), 0) & d) == 0
            part = jnp.where(low, a, b) + pltpu.roll(jnp.where(low, b, a), 8 - d, 0)
            level += 1
        self.held.append((part, level))

    def result(self):
        return self.held[0][0]


def load_decay(weights_ref):
    rows = weights_ref[128:144, :].astype(f32)
    return [(-LOG2E) * jnp.exp(rows[:, tile_of(j)]) for j in range(TILES)]


def load_state(ref):
    state = ref[...].reshape(STATE, CB)
    return tuple(state[:, tile_of(j)] for j in range(TILES))


def aligned(tb):
    return pl.ds(pl.multiple_of(tb * 8, 8), 8)


ZERO_STATE = (STATE, LANES)


def end_state_kernel(step_ref, conv_ref, b_ref, weights_ref, out_ref):
    decay = load_decay(weights_ref)

    def block(tb, hs):
        hs = list(hs)
        dt8 = step_ref[0, aligned(tb), :]
        u8 = dt8 * conv_ref[0, aligned(tb), :]
        for i in range(8):
            b = b_ref[0, tb * 8 + i]
            for j in range(TILES):
                dt = dt8[i : i + 1, tile_of(j)]
                u = u8[i : i + 1, tile_of(j)]
                hs[j] = jnp.exp2(dt * decay[j]) * hs[j] + b * u
        return tuple(hs)

    zero = jnp.zeros(ZERO_STATE, f32)
    hs = lax.fori_loop(0, TOK // 8, block, (zero,) * TILES)
    total = jnp.sum(step_ref[0], axis=0, keepdims=True)
    for j in range(TILES):
        prod = jnp.exp2(total[:, tile_of(j)] * decay[j])
        out_ref[:, :, tile_of(j)] = prod.reshape(STATE, 1, LANES)
        out_ref[:, :, tile_of(j + TILES)] = hs[j].reshape(STATE, 1, LANES)


def scan_kernel(
    step_ref, conv_ref, b_ref, c_ref, weights_ref, start_ref, act_ref, my_ref, gated_ref
):
    decay = load_decay(weights_ref)
    skip = weights_ref[144:152, :].astype(f32)[6:7]

    def block(tb, hs):
        hs = list(hs)
        dt8 = step_ref[0, aligned(tb), :]
        conv8 = conv_ref[0, aligned(tb), :]
        u8 = dt8 * conv8
        outs = [Fold() for _ in range(TILES)]
        for i in range(8):
            t = tb * 8 + i
            b = b_ref[0, t]
            c = c_ref[0, t]
            for j in range(TILES):
                dt = dt8[i : i + 1, tile_of(j)]
                u = u8[i : i + 1, tile_of(j)]
                hs[j] = jnp.exp2(dt * decay[j]) * hs[j] + b * u
                outs[j].add(hs[j] * c)
        for j in range(TILES):
            my_ref[0, aligned(tb), tile_of(j)] = (
                outs[j].result() + skip[:, tile_of(j)] * conv8[:, tile_of(j)]
            )
        return tuple(hs)

    lax.fori_loop(0, TOK // 8, block, load_state(start_ref))
    gated_ref[0] = (my_ref[0] * act_ref[0]).astype(bf16)


def history_kernel(step_ref, conv_ref, b_ref, weights_ref, start_ref, before_ref, ah_ref):
    decay = load_decay(weights_ref)

    def block(tb, hs):
        hs = list(hs)
        dt8 = step_ref[0, aligned(tb), :]
        u8 = dt8 * conv_ref[0, aligned(tb), :]
        for i in range(8):
            t = tb * 8 + i
            b = b_ref[0, t]
            for j in range(TILES):
                dt = dt8[i : i + 1, tile_of(j)]
                u = u8[i : i + 1, tile_of(j)]
                ah = jnp.exp2(dt * decay[j]) * hs[j]
                ah_ref[0, t, :, tile_of(j)] = ah
                hs[j] = ah + b * u
        return tuple(hs)

    lax.fori_loop(0, TOK // 8, block, load_state(start_ref))


def end_adjoint_kernel(step_ref, gy_ref, c_ref, weights_ref, mu_ref):
    decay = load_decay(weights_ref)

    def block(k, mus):
        mus = list(mus)
        tb = TOK // 8 - 1 - k
        dt8 = step_ref[0, aligned(tb), :]
        gy8 = gy_ref[0, aligned(tb), :]
        for i in reversed(range(8)):
            c = c_ref[0, tb * 8 + i]
            for j in range(TILES):
                dt = dt8[i : i + 1, tile_of(j)]
                gy = gy8[i : i + 1, tile_of(j)]
                mus[j] = jnp.exp2(dt * decay[j]) * (mus[j] + c * gy)
        return tuple(mus)

    zero = jnp.zeros(ZERO_STATE, f32)
    mus = lax.fori_loop(0, TOK // 8, block, (zero,) * TILES)
    for j in range(TILES):
        mu_ref[:, :, tile_of(j)] = mus[j].reshape(STATE, 1, LANES)


def scan_back_kernel(
    step_ref,
    sig_ref,
    conv_ref,
    gy_ref,
    ah_ref,
    b_ref,
    c_ref,
    weights_ref,
    later_ref,
    cin_ref,
    low_ref,
    maps_ref,
    first_ref,
    gcin_ref,
    halo_ref,
    second_ref,
    glow_ref,
    guy_ref,
    s1_ref,
    s2_ref,
    gb_ref,
    gc_ref,
):
    phase = pl.program_id(1)

    @pl.when(phase == 0)
    def _():
        gb_ref[...] = jnp.zeros_like(gb_ref)
        gc_ref[...] = jnp.zeros_like(gc_ref)
        glow_ref[...] = jnp.zeros_like(glow_ref)
        guy_ref[...] = jnp.zeros_like(guy_ref)

    @pl.when(phase < NCB)
    def _():
        decay = load_decay(weights_ref)

        def backward(k, carry):
            mus, gds = list(carry[0]), list(carry[1])
            tb = TOK // 8 - 1 - k
            dt8 = step_ref[0, aligned(tb), :]
            u8 = dt8 * conv_ref[0, aligned(tb), :]
            gy8 = gy_ref[0, aligned(tb), :]
            out1 = [Fold(True) for _ in range(TILES)]
            out2 = [Fold(True) for _ in range(TILES)]
            for i in reversed(range(8)):
                t = tb * 8 + i
                b = b_ref[0, t]
                c = c_ref[0, t]
                gb = gb_ref[t]
                gc = gc_ref[t]
                for j in range(TILES):
                    dt = dt8[i : i + 1, tile_of(j)]
                    u = u8[i : i + 1, tile_of(j)]
                    gy = gy8[i : i + 1, tile_of(j)]
                    ah = ah_ref[0, t, :, tile_of(j)]
                    z = dt * decay[j]
                    lam = c * gy + mus[j]
                    w = lam * ah * z
                    out1[j].add(lam * b)
                    out2[j].add(w)
                    gds[j] = gds[j] + w
                    gb = gb + lam * u
                    gc = gc + gy * ah
                    mus[j] = jnp.exp2(z) * lam
                gb_ref[t] = gb
                gc_ref[t] = gc
            for j in range(TILES):
                s1_ref[phase, aligned(tb), tile_of(j)] = out1[j].result()
                s2_ref[aligned(tb), tile_of(j)] = out2[j].result()
            return tuple(mus), tuple(gds)

        zero = jnp.zeros(ZERO_STATE, f32)
        _, gds = lax.fori_loop(
            0, TOK // 8, backward, (load_state(later_ref), (zero,) * TILES)
        )
        for j in range(TILES):
            first_ref[0, 48:64, tile_of(j)] = LN2 * gds[j]
        step, conv, sig = step_ref[0], conv_ref[0], sig_ref[0]
        share = jnp.where(step > 1e-30, sig / jnp.maximum(step, 1e-30), 1.0)
        gsp = LN2 * s2_ref[...] * share + conv * s1_ref[phase] * sig
        guy_ref[...] += jnp.sum(gy_ref[0] * step * conv, axis=1, keepdims=True)
        gsp_low = gsp.astype(bf16)
        first_ref[0, 0:48, :] = dot(low_ref[0], gsp_low, 0, 0)
        first_ref[0, 64:72, :] = jnp.broadcast_to(
            jnp.sum(gsp, axis=0, keepdims=True), (8, CB)
        )
        glow_ref[:, 0:48] += dot(gsp_low, weights_ref[80:128, :], 1, 1)

    @pl.when(phase == NCB)
    def _():
        glow_ref[:, 48:64] = jnp.sum(gb_ref[...], axis=-1)
        glow_ref[:, 64:80] = jnp.sum(gc_ref[...], axis=-1) + guy_ref[...] * maps_ref[0, :, 48:64]

    @pl.when(phase >= NCB)
    def _():
        gy = gy_ref[0]
        conv = conv_ref[0]
        vecs = weights_ref[144:152, :].astype(f32)
        glow = glow_ref[...].astype(bf16)
        gconv = (
            step_ref[0] * s1_ref[phase - NCB]
            + vecs[6:7] * gy
            + dot(glow, weights_ref[0:80, :], 1, 0)
        )
        second_ref[0, 0:80, :] = dot(glow, conv.astype(bf16), 0, 0)
        cin = cin_ref[0].astype(f32)
        first = HEAD - CONV + 1
        pieces = [cin[first + i : first + i + TOK] for i in range(CONV)]
        v = vecs[4:5] + sum(vecs[i : i + 1] * pieces[i] for i in range(CONV))
        gv = gconv * silu_parts(v)[1]
        for i in range(CONV):
            second_ref[0, 80 + i : 81 + i, :] = jnp.sum(gv * pieces[i], axis=0, keepdims=True)
        second_ref[0, 84:85, :] = jnp.sum(gv, axis=0, keepdims=True)
        second_ref[0, 85:86, :] = jnp.sum(gy * conv, axis=0, keepdims=True)
        second_ref[0, 86:88, :] = jnp.zeros((2, CB), f32)
        edge = jnp.zeros((8, CB), f32)
        padded = jnp.concatenate([edge, gv, edge], axis=0)
        gcin = sum(
            vecs[i : i + 1] * padded[CONV - 1 - i : CONV - 1 - i + TOK + HEAD]
            for i in range(CONV)
        )
        halo_ref[0] = gcin[:HEAD]
        gcin_ref[0] = gcin[HEAD:]


def same(c):
    return c


def at(c):
    return jnp.minimum(c, NCB - 1)


def wrap(c):
    return lax.rem(c, NCB)


def second(c):
    return jnp.maximum(c - NCB, 0)


def token_spec(place=same, rows=TOK):
    return pl.BlockSpec((1, rows, CB), lambda m, c: (m, 0, place(c)))


def weights_spec(place=same):
    return pl.BlockSpec((WEIGHT_ROWS, CB), lambda m, c: (0, place(c)))


ANYWHERE = pl.BlockSpec(memory_space=pl.ANY)
MAP_SPEC = pl.BlockSpec((1, TOK, STATE, LANES), lambda m, c: (m, 0, 0, 0))


def state_spec(width=CB, place=same):
    return pl.BlockSpec((STATE, 1, width), lambda m, c: (m * NCB + place(c), 0, 0))


def history_spec(place=same):
    return pl.BlockSpec((1, TOK, STATE, CB), lambda m, c: (m, 0, 0, place(c)))


def shape_of(*shape, dtype=f32):
    return jax.ShapeDtypeStruct(shape, dtype)


PARAMS = pltpu.CompilerParams(
    dimension_semantics=("arbitrary", "arbitrary"), vmem_limit_bytes=48 * MIB
)


def lasting(us):
    return pl.CostEstimate(flops=us * 10**9, bytes_accessed=us * 3 * 10**6, transcendentals=0)


def end_state(step, conv, in_map, weights):
    return pl.pallas_call(
        end_state_kernel,
        grid=(MICRO, NCB),
        in_specs=[token_spec(), token_spec(), MAP_SPEC, weights_spec()],
        out_specs=state_spec(2 * CB),
        out_shape=shape_of(DEVICES, 1, 2 * CB),
        compiler_params=PARAMS,
        cost_estimate=lasting(6),
        name="end_state",
    )(step, conv, in_map, weights)


def scan(step, conv, in_map, out_map, weights, start, act):
    return pl.pallas_call(
        scan_kernel,
        grid=(MICRO, NCB),
        in_specs=[
            token_spec(),
            token_spec(),
            MAP_SPEC,
            MAP_SPEC,
            weights_spec(),
            state_spec(),
            token_spec(),
        ],
        out_specs=[token_spec(), token_spec()],
        out_shape=[shape_of(MICRO, TOK, DI), shape_of(MICRO, TOK, DI, dtype=bf16)],
        compiler_params=PARAMS,
        cost_estimate=lasting(12),
        name="scan",
    )(step, conv, in_map, out_map, weights, start, act)


def history(step, conv, in_map, weights, start, before):
    return pl.pallas_call(
        history_kernel,
        grid=(MICRO, NCB),
        in_specs=[token_spec(), token_spec(), MAP_SPEC, weights_spec(), state_spec(), ANYWHERE],
        out_specs=history_spec(),
        out_shape=shape_of(MICRO, TOK, STATE, DI),
        compiler_params=PARAMS,
        cost_estimate=lasting(12),
        name="history",
    )(step, conv, in_map, weights, start, before)


def end_adjoint(step, gy, out_map, weights):
    return pl.pallas_call(
        end_adjoint_kernel,
        grid=(MICRO, NCB),
        in_specs=[token_spec(), token_spec(), MAP_SPEC, weights_spec()],
        out_specs=state_spec(),
        out_shape=shape_of(DEVICES, 1, CB),
        compiler_params=PARAMS,
        cost_estimate=lasting(6),
        name="end_adjoint",
    )(step, gy, out_map, weights)


def scan_back(step, sig, conv, gy, ah, in_map, out_map, weights, later, cin, low, maps):
    return pl.pallas_call(
        scan_back_kernel,
        grid=(MICRO, 2 * NCB),
        in_specs=[
            token_spec(wrap),
            token_spec(at),
            token_spec(wrap),
            token_spec(wrap),
            history_spec(at),
            MAP_SPEC,
            MAP_SPEC,
            weights_spec(wrap),
            state_spec(CB, at),
            token_spec(second, TOK + HEAD),
            pl.BlockSpec((1, TOK, RANK), lambda m, c: (m, 0, 0)),
            pl.BlockSpec((1, TOK, 80), lambda m, c: (m, 0, 0)),
        ],
        out_specs=[
            token_spec(at, 72),
            token_spec(second),
            token_spec(second, HEAD),
            token_spec(second, 88),
        ],
        out_shape=[
            shape_of(MICRO, 72, DI),
            shape_of(MICRO, TOK, DI),
            shape_of(MICRO, HEAD, DI),
            shape_of(MICRO, 88, DI),
        ],
        scratch_shapes=[
            pltpu.VMEM((TOK, 80), f32),
            pltpu.VMEM((TOK, 1), f32),
            pltpu.VMEM((NCB, TOK, CB), f32),
            pltpu.VMEM((TOK, CB), f32),
            pltpu.VMEM((TOK, STATE, LANES), f32),
            pltpu.VMEM((TOK, STATE, LANES), f32),
        ],
        compiler_params=PARAMS,
        cost_estimate=lasting(36),
        name="scan_back",
    )(step, sig, conv, gy, ah, in_map, out_map, weights, later, cin, low, maps)


def prefix_kernel(reverse, prod_ref, state_ref, before_ref, out_ref):
    skipped = state_ref.shape[2] - CB

    def one(k, state):
        i = DEVICES - 1 - k if reverse else k
        out_ref[i] = state
        return prod_ref[i, :, :CB] * state + state_ref[i, :, skipped:]

    lax.fori_loop(0, DEVICES, one, jnp.zeros((1, CB), f32), unroll=8)


def prefix(prod, state, reverse, before):
    return pl.pallas_call(
        partial(prefix_kernel, reverse),
        in_specs=[pl.BlockSpec(memory_space=pltpu.VMEM)] * 2 + [ANYWHERE],
        out_shape=shape_of(DEVICES, 1, CB),
        cost_estimate=lasting(2),
        name="prefix",
    )(prod, state, before)


ROWS = EXPERTS * MICRO * CAP
FB = 768
NFB = FF // FB
EXP_PARAMS = pltpu.CompilerParams(
    dimension_semantics=("arbitrary",), vmem_limit_bytes=56 * MIB
)


def gelu_parts(v):
    c = 0.7978845608028654
    v2 = v * v
    th = jnp.tanh(c * (v + 0.044715 * v * v2))
    half = 0.5 * (1.0 + th)
    return v * half, half + 0.5 * v * (1.0 - th * th) * c * (1.0 + 3 * 0.044715 * v2)


def expert_kernel(rows_ref, up_ref, down_ref, before_ref, hidden_ref, gpre_ref, out_ref, acc_ref):
    j = pl.program_id(0)
    up = up_ref[...].reshape(D, FB)
    down = down_ref[...].reshape(FB, D)
    x = rows_ref[:, :D]
    g = rows_ref[:, D:]
    act, slope = gelu_parts(dot(x, up, 1, 0))
    hidden = act.astype(bf16)
    gpre = (dot(g, down, 1, 1) * slope).astype(bf16)
    hidden_ref[...] = hidden
    gpre_ref[...] = gpre
    eo = dot(hidden, down, 1, 0)
    gr = dot(gpre, up, 1, 1)

    @pl.when(j == 0)
    def _():
        acc_ref[:, :D] = eo
        acc_ref[:, D:] = gr

    @pl.when(j > 0)
    def _():
        acc_ref[:, :D] += eo
        acc_ref[:, D:] += gr

    @pl.when(j == NFB - 1)
    def _():
        out_ref[...] = acc_ref[...].astype(bf16)


def expert_call(rows, weights, before):
    return pl.pallas_call(
        expert_kernel,
        grid=(NFB,),
        in_specs=[
            pl.BlockSpec((ROWS, 2 * D), lambda j: (0, 0)),
            pl.BlockSpec((16, 48, D), lambda j: (0, j, 0)),
            pl.BlockSpec((4, 192, D), lambda j: (j, 1, 0)),
            ANYWHERE,
        ],
        out_specs=[
            pl.BlockSpec((ROWS, FB), lambda j: (0, j)),
            pl.BlockSpec((ROWS, FB), lambda j: (0, j)),
            pl.BlockSpec((ROWS, 2 * D), lambda j: (0, 0)),
        ],
        out_shape=[
            jax.ShapeDtypeStruct((ROWS, FF), bf16),
            jax.ShapeDtypeStruct((ROWS, FF), bf16),
            jax.ShapeDtypeStruct((ROWS, 2 * D), bf16),
        ],
        scratch_shapes=[pltpu.VMEM((ROWS, 2 * D), f32)],
        compiler_params=EXP_PARAMS,
        cost_estimate=lasting(11),
        name="expert",
    )(rows, weights, weights, before)


def expert_grad_kernel(rows_ref, hidden_ref, gpre_ref, out_ref):
    j = pl.program_id(0)
    gup = dot(rows_ref[:, :D], gpre_ref[...], 0, 0).astype(bf16)
    gdown = dot(hidden_ref[...], rows_ref[:, D:], 0, 0).astype(bf16)
    out_ref[:, pl.ds(pl.multiple_of(j * 48, 16), 48), :] = gup.reshape(16, 48, D)
    out_ref[pl.ds(j * 4, 4), 192:384, :] = gdown.reshape(4, 192, D)


def expert_grad_call(rows, hidden, gpre):
    return pl.pallas_call(
        expert_grad_kernel,
        grid=(NFB,),
        in_specs=[
            pl.BlockSpec((ROWS, 2 * D), lambda j: (0, 0)),
            pl.BlockSpec((ROWS, FB), lambda j: (0, j)),
            pl.BlockSpec((ROWS, FB), lambda j: (0, j)),
        ],
        out_specs=pl.BlockSpec((16, 384, D), lambda j: (0, 0, 0)),
        out_shape=shape_of(16, 576, D, dtype=bf16),
        compiler_params=EXP_PARAMS,
        cost_estimate=lasting(11),
        name="expert_grad",
    )(rows, hidden, gpre)


def picks(natural, size):
    shape = (size, natural.shape[1])
    return (lax.broadcasted_iota(jnp.int32, shape, 0) == natural).astype(bf16)


def split_dot(a, b):
    high = a.astype(bf16)
    low = (a - high.astype(f32)).astype(bf16)
    return dot(high, b, 1, 1) + dot(low, b, 1, 1)


def early_grad_kernel(held_ref, gated_ref, mix_ref, normed_ref, branch_ref, before_ref, out_ref):
    out_ref[:, 0:96, :] = dot(gated_ref[...], mix_ref[...], 0, 0).astype(bf16).reshape(16, 96, D)
    for h in range(2):
        part = dot(normed_ref[...], branch_ref[:, h * D : (h + 1) * D], 0, 0)
        out_ref[:, 96 + 48 * h : 144 + 48 * h, :] = part.astype(bf16).reshape(16, 48, D)


def early_grad_call(held, gated, mix, normed, branch, before):
    return pl.pallas_call(
        early_grad_kernel,
        grid=(1,),
        in_specs=[
            pl.BlockSpec(memory_space=pl.ANY),
            pl.BlockSpec((MICRO * TOK, DI), lambda j: (0, 0)),
            pl.BlockSpec((MICRO * TOK, D), lambda j: (0, 0)),
            pl.BlockSpec((MICRO * TOK, D), lambda j: (0, 0)),
            pl.BlockSpec((MICRO * TOK, DI), lambda j: (0, 0)),
            ANYWHERE,
        ],
        out_specs=pl.BlockSpec((16, 192, D), lambda j: (0, 2, 0)),
        out_shape=shape_of(16, 576, D, dtype=bf16),
        input_output_aliases={0: 0},
        compiler_params=EXP_PARAMS,
        cost_estimate=lasting(12),
        name="early_grad",
    )(held, gated, mix, normed, branch, before)


def rows_kernel(first, state_ref, before_ref, out_ref):
    for m in range(MICRO):
        part = state_ref[m][:, first : first + STATE]
        out_ref[m] = jnp.broadcast_to(part[:, :, None], (TOK, STATE, LANES))


def rows_call(first, state, before):
    return pl.pallas_call(
        partial(rows_kernel, first),
        in_specs=[pl.BlockSpec(memory_space=pltpu.VMEM), ANYWHERE],
        out_shape=shape_of(MICRO, TOK, STATE, LANES),
        compiler_params=pltpu.CompilerParams(vmem_limit_bytes=32 * MIB),
        cost_estimate=lasting(12),
        name="rows",
    )(state, before)


def gathered_row(k, rows):
    return (k % (16 * rows) // rows * 8 + k // (16 * rows)) * rows + k % rows


def gate_kernel(normed_ref, late_ref, before_ref, act_ref, slope_ref, out_ref, total_ref):
    j = pl.program_id(0)
    act, slope = silu_parts(dot(normed_ref[...], late_ref[:, :D], 1, 0))
    act_ref[...] = act
    slope_ref[...] = slope
    k = lax.broadcasted_iota(jnp.int32, (1, D), 1)
    source = (k % 96 // 6 * 8 + k // 96) * 12 + j * 6 + k % 6
    part = dot(picks(source, DI), late_ref[:, D:], 1, 0)

    @pl.when(j == 0)
    def _():
        total_ref[...] = part

    @pl.when(j == 1)
    def _():
        out_ref[...] = (total_ref[...] + part).astype(bf16)


def gate_call(normed, late, before):
    return pl.pallas_call(
        gate_kernel,
        grid=(2,),
        in_specs=[
            pl.BlockSpec((MICRO * TOK, D), lambda j: (0, 0)),
            pl.BlockSpec((D, DI), lambda j: (0, j)),
            ANYWHERE,
        ],
        out_specs=[
            pl.BlockSpec((MICRO * TOK, D), lambda j: (0, j)),
            pl.BlockSpec((MICRO * TOK, D), lambda j: (0, j)),
            pl.BlockSpec((DI, D), lambda j: (0, 0)),
        ],
        out_shape=[
            shape_of(MICRO * TOK, DI),
            shape_of(MICRO * TOK, DI),
            shape_of(DI, D, dtype=bf16),
        ],
        scratch_shapes=[pltpu.VMEM((DI, D), f32)],
        compiler_params=EXP_PARAMS,
        cost_estimate=lasting(12),
        name="gate",
    )(normed, late, before)


def front_kernel(
    x_ref,
    gain_ref,
    in_c_ref,
    weights_ref,
    nat_ref,
    normed_ref,
    cin_ref,
    conv_ref,
    state_ref,
    low_ref,
    step_ref,
    sig_ref,
    rows_ref,
):
    phase = pl.program_id(0)

    @pl.when(phase == 0)
    def _():
        x = x_ref[...].astype(f32).reshape(MICRO * (TOK + HEAD), D)
        scale = lax.rsqrt(jnp.mean(x * x, axis=-1, keepdims=True) + EPSILON)
        nat = (x * scale * gain_ref[...]).astype(bf16)
        k = lax.broadcasted_iota(jnp.int32, (1, D), 1)
        rows_ref[...] = dot(nat, picks(gathered_row(k, 6), D), 1, 0).astype(bf16)
        for m in range(MICRO):
            first = m * (TOK + HEAD) + HEAD
            nat_ref[m * TOK : (m + 1) * TOK, :] = nat[first : first + TOK]
            normed_ref[m * TOK : (m + 1) * TOK, :] = rows_ref[first : first + TOK, :]
        state_ref[...] = jnp.zeros_like(state_ref)

    @pl.when(phase < NCB)
    def _():
        vecs = weights_ref[144:152, :].astype(f32)
        cin = dot(rows_ref[...], in_c_ref[...], 1, 0).astype(bf16).reshape(MICRO, TOK + HEAD, CB)
        cin_ref[...] = cin
        first = HEAD - CONV + 1
        for m in range(MICRO):
            rows = cin[m].astype(f32)
            v = vecs[4:5] + sum(
                vecs[i : i + 1] * rows[first + i : first + i + TOK] for i in range(CONV)
            )
            conv = silu_parts(v)[0].astype(bf16)
            conv_ref[m] = conv.astype(f32)
            state_ref[m] += dot(conv, weights_ref[0:80, :], 1, 1)

    @pl.when(phase == NCB)
    def _():
        low_ref[...] = state_ref[:, :, :RANK].astype(bf16)

    @pl.when(phase >= NCB)
    def _():
        bias = weights_ref[144:152, :].astype(f32)[5:6]
        for m in range(MICRO):
            pre = dot(low_ref[m], weights_ref[80:128, :], 1, 0) + bias
            step_ref[m] = jax.nn.softplus(pre)
            sig_ref[m] = jax.nn.sigmoid(pre)


def front_call(x, gain, in_c, weights):
    def blocks(rows, place):
        return pl.BlockSpec((MICRO, rows, CB), lambda c: (0, 0, place(c)))

    def whole(*shape):
        return pl.BlockSpec(shape, lambda c: (0,) * len(shape))

    return pl.pallas_call(
        front_kernel,
        grid=(2 * NCB,),
        in_specs=[
            whole(MICRO, TOK + HEAD, D),
            whole(1, D),
            pl.BlockSpec((D, CB), lambda c: (0, at(c))),
            pl.BlockSpec((WEIGHT_ROWS, CB), lambda c: (0, wrap(c))),
        ],
        out_specs=[
            whole(MICRO * TOK, D),
            whole(MICRO * TOK, D),
            blocks(TOK + HEAD, at),
            blocks(TOK, at),
            whole(MICRO, TOK, 80),
            whole(MICRO, TOK, RANK),
            blocks(TOK, second),
            blocks(TOK, second),
        ],
        out_shape=[
            shape_of(MICRO * TOK, D, dtype=bf16),
            shape_of(MICRO * TOK, D, dtype=bf16),
            shape_of(MICRO, TOK + HEAD, DI, dtype=bf16),
            shape_of(MICRO, TOK, DI),
            shape_of(MICRO, TOK, 80),
            shape_of(MICRO, TOK, RANK, dtype=bf16),
            shape_of(MICRO, TOK, DI),
            shape_of(MICRO, TOK, DI),
        ],
        scratch_shapes=[pltpu.VMEM((MICRO * (TOK + HEAD), D), bf16)],
        compiler_params=EXP_PARAMS,
        cost_estimate=lasting(8),
        name="front",
    )(x, gain, in_c, weights)


def owned_rows(core, normed, low_ref, small_ref, out_ref):
    k = lax.broadcasted_iota(jnp.int32, (1, 512), 1)
    row = k % 8
    inner = picks(jnp.where(row < 6, (k // 8 * 2 + core) * 6 + row, -1), D)
    inner = dot(normed, inner, 1, 0).astype(bf16)
    outer = picks(jnp.where(row < 6, -1, (k // 8 * 2 + core) * 2 + row - 6), 2 * DEVICES)
    for j in range(2):
        columns = slice(j * D, (j + 1) * D)
        part = dot(inner, low_ref[:, columns], 0, 0) + dot(outer, small_ref[:, columns], 0, 0)
        out_ref[:, columns] = part.astype(bf16)


def dispatch_kernel(
    gated_ref,
    out_w_ref,
    x_ref,
    gain_ref,
    router_ref,
    hot_ref,
    table_ref,
    grad_ref,
    residual_ref,
    gate_ref,
    probs_ref,
    sent_ref,
):
    part = dot(gated_ref[...], out_w_ref[...], 1, 0)

    @pl.when(pl.program_id(0) == 0)
    def _():
        residual_ref[...] = x_ref[...].astype(f32) + part

    @pl.when(pl.program_id(0) > 0)
    def _():
        residual_ref[...] += part

    @pl.when(pl.program_id(0) == NCB - 1)
    def _():
        residual = residual_ref[...]
        scale = lax.rsqrt(jnp.mean(residual * residual, axis=-1, keepdims=True) + EPSILON)
        normed = (residual * scale * gain_ref[...]).astype(bf16)
        logits = dot(normed, router_ref[...], 1, 1)
        powers = jnp.exp(logits - jnp.max(logits, axis=-1, keepdims=True))
        probs = powers / jnp.sum(powers, axis=-1, keepdims=True)
        gate = jnp.sum(probs * hot_ref[...], axis=-1, keepdims=True)
        probs_ref[...] = probs
        gate_ref[...] = gate
        sent_ref[:, :D] = dot(table_ref[...], normed, 1, 0).astype(bf16)
        grad = (gate * grad_ref[...].astype(f32)).astype(bf16)
        sent_ref[:, D:] = dot(table_ref[...], grad, 1, 0).astype(bf16)


def dispatch_call(gated, out_w, x, gain, router, hot, table, grad):
    tokens = MICRO * TOK

    def whole(*shape):
        return pl.BlockSpec(shape, lambda c: (0, 0))

    return pl.pallas_call(
        dispatch_kernel,
        grid=(NCB,),
        in_specs=[
            pl.BlockSpec((tokens, CB), lambda c: (0, c)),
            pl.BlockSpec((CB, D), lambda c: (c, 0)),
            whole(tokens, D),
            whole(1, D),
            whole(EXPERTS, D),
            whole(tokens, EXPERTS),
            whole(ROWS, tokens),
            whole(tokens, D),
        ],
        out_specs=[
            whole(tokens, D),
            whole(tokens, 1),
            whole(tokens, EXPERTS),
            whole(ROWS, 2 * D),
        ],
        out_shape=[
            shape_of(tokens, D),
            shape_of(tokens, 1),
            shape_of(tokens, EXPERTS),
            shape_of(ROWS, 2 * D, dtype=bf16),
        ],
        compiler_params=EXP_PARAMS,
        cost_estimate=lasting(4),
        name="dispatch",
    )(gated, out_w, x, gain, router, hot, table, grad)


def combine_kernel(
    table_ref,
    back_ref,
    residual_ref,
    gate_ref,
    probs_ref,
    hot_ref,
    grad_ref,
    router_ref,
    gain_ref,
    out_w_ref,
    act_ref,
    slope_ref,
    my_ref,
    before_ref,
    mixed_ref,
    grad_residual_ref,
    mix_ref,
    gy_ref,
    branch_ref,
    wide_ref,
):
    @pl.when(pl.program_id(0) == 0)
    def _():
        returned = dot(table_ref[...], back_ref[...], 0, 0)
        expert_out, grad_in = returned[:, :D], returned[:, D:]
        residual, gate, grad = residual_ref[...], gate_ref[...], grad_ref[...].astype(f32)
        mixed_ref[...] = (residual + gate * expert_out).astype(bf16)
        grad_gate = jnp.sum(grad * expert_out, axis=-1, keepdims=True)
        grad_logits = grad_gate * gate * (hot_ref[...] - probs_ref[...])
        high = grad_logits.astype(bf16)
        low = (grad_logits - high.astype(f32)).astype(bf16)
        grad_in = grad_in + dot(high, router_ref[...], 1, 0) + dot(low, router_ref[...], 1, 0)
        scale = lax.rsqrt(jnp.mean(residual * residual, axis=-1, keepdims=True) + EPSILON)
        unit = residual * scale
        normed = (unit * gain_ref[...]).astype(bf16)
        wide_ref[0:1, :] = jnp.sum(grad_in * unit, axis=0, keepdims=True)
        wide_ref[1:9, :] = dot(high, normed, 0, 0) + dot(low, normed, 0, 0)
        wide_ref[9:16, :] = jnp.zeros((7, D), f32)
        scaled = grad_in * gain_ref[...]
        grad = grad + scale * (scaled - unit * jnp.mean(scaled * unit, axis=-1, keepdims=True))
        grad_residual_ref[...] = grad
        mix_ref[...] = grad.astype(bf16)

    grad = dot(mix_ref[...], out_w_ref[...], 1, 1)
    gy_ref[...] = grad * act_ref[...]
    branch_ref[...] = (grad * my_ref[...] * slope_ref[...]).astype(bf16)


def combine_call(table, back, residual, gate, probs, hot, grad, router, gain, out_w, act, slope, my, before):
    tokens = MICRO * TOK

    def whole(*shape):
        return pl.BlockSpec(shape, lambda c: (0, 0))

    columns = pl.BlockSpec((tokens, CB), lambda c: (0, c))
    return pl.pallas_call(
        combine_kernel,
        grid=(NCB,),
        in_specs=[
            whole(ROWS, tokens),
            whole(ROWS, 2 * D),
            whole(tokens, D),
            whole(tokens, 1),
            whole(tokens, EXPERTS),
            whole(tokens, EXPERTS),
            whole(tokens, D),
            whole(EXPERTS, D),
            whole(1, D),
            pl.BlockSpec((CB, D), lambda c: (c, 0)),
            columns,
            columns,
            columns,
            ANYWHERE,
        ],
        out_specs=[
            whole(tokens, D),
            whole(tokens, D),
            whole(tokens, D),
            columns,
            columns,
            whole(16, D),
        ],
        out_shape=[
            shape_of(tokens, D, dtype=bf16),
            shape_of(tokens, D),
            shape_of(tokens, D, dtype=bf16),
            shape_of(tokens, DI),
            shape_of(tokens, DI, dtype=bf16),
            shape_of(16, D),
        ],
        compiler_params=EXP_PARAMS,
        cost_estimate=lasting(6),
        name="combine",
    )(table, back, residual, gate, probs, hot, grad, router, gain, out_w, act, slope, my, before)


def other_grad_kernel(place_ref, cin_ref, next_ref, normed_ref, small_ref, low_ref, out_ref):
    for m in range(MICRO):
        low_ref[m * TOK : (m + 1) * TOK - 16, :] = cin_ref[m, : TOK - 16, :].astype(bf16)
        last = jnp.concatenate(
            [cin_ref[m, TOK - 16 : TOK - 8, :], cin_ref[m, TOK - 8 :, :] + next_ref[m]], axis=0
        )
        low_ref[(m + 1) * TOK - 16 : (m + 1) * TOK, :] = last.astype(bf16)
    owned_rows(1 - place_ref[1], normed_ref[...], low_ref, small_ref, out_ref)


def other_grad_call(place, cin, following, normed, small):
    vmem = pl.BlockSpec(memory_space=pltpu.VMEM)
    return pl.pallas_call(
        other_grad_kernel,
        in_specs=[pl.BlockSpec(memory_space=pltpu.SMEM)] + [vmem] * 4,
        out_specs=[vmem] * 2,
        out_shape=[
            shape_of(MICRO * TOK, DI, dtype=bf16),
            shape_of(512, DI, dtype=bf16),
        ],
        compiler_params=pltpu.CompilerParams(vmem_limit_bytes=48 * MIB),
        cost_estimate=lasting(6),
        name="other_grad",
    )(place, cin, following, normed, small)


def own_grad_kernel(place_ref, low_ref, normed_ref, small_ref, out_ref):
    owned_rows(place_ref[1], normed_ref[...], low_ref, small_ref, out_ref)


def own_grad_call(place, low, normed, small):
    vmem = pl.BlockSpec(memory_space=pltpu.VMEM)
    return pl.pallas_call(
        own_grad_kernel,
        in_specs=[pl.BlockSpec(memory_space=pltpu.SMEM)] + [vmem] * 3,
        out_specs=vmem,
        out_shape=shape_of(512, DI, dtype=bf16),
        compiler_params=pltpu.CompilerParams(vmem_limit_bytes=48 * MIB),
        cost_estimate=lasting(6),
        name="own_grad",
    )(place, low, normed, small)


def input_grad_kernel(
    cin_ref,
    branch_ref,
    in_c_ref,
    late_ref,
    x_ref,
    gain_ref,
    residual_ref,
    before_ref,
    out_ref,
):
    k = lax.broadcasted_iota(jnp.int32, (1, D), 1)
    grad = dot(cin_ref[...], in_c_ref[...], 1, 1)
    for h in range(2):
        grad += dot(
            branch_ref[:, h * D : (h + 1) * D], late_ref[:, 2 * h * D : (2 * h + 1) * D], 1, 1
        )
    scaled = split_dot(grad, picks(gathered_row(k, 6), D)) * gain_ref[...]
    x = x_ref[...]
    scale = lax.rsqrt(jnp.mean(x * x, axis=-1, keepdims=True) + EPSILON)
    unit = x * scale
    out_ref[...] = residual_ref[...] + scale * (
        scaled - unit * jnp.mean(scaled * unit, axis=-1, keepdims=True)
    )


def input_grad_call(*args):
    return pl.pallas_call(
        input_grad_kernel,
        in_specs=[pl.BlockSpec(memory_space=pltpu.VMEM)] * 7 + [ANYWHERE],
        out_shape=shape_of(MICRO * TOK, D),
        compiler_params=pltpu.CompilerParams(vmem_limit_bytes=56 * MIB),
        cost_estimate=lasting(20),
        name="input_grad",
    )(*args)


def shares_kernel(place_ref, big_ref, before_ref, up_ref, down_ref, own_ref, other_ref):
    for j in range(NFB):
        up_ref[:, j * FB : (j + 1) * FB] = big_ref[j * 48 : (j + 1) * 48, :].astype(f32)
    down_ref[...] = big_ref[192:384, :].astype(f32)
    k = lax.broadcasted_iota(jnp.int32, (1, 96), 1)
    piece, row = k // 24, k % 24
    chip = (place_ref[0] + jnp.where(piece == 1, 3, jnp.where(piece == 2, 1, piece - piece // 3))) % CHIPS
    for core, ref in ((place_ref[1], own_ref), (1 - place_ref[1], other_ref)):
        owner = 2 * chip + core
        source = jnp.where(row < 12, owner * 12 + row, 96 + row // 18 * 48 + owner * 6 + row % 6)
        ref[...] = dot(picks(source, 192), big_ref[384:576, :], 0, 0).astype(bf16)


def shares_call(place, big, before):
    vmem = pl.BlockSpec(memory_space=pltpu.VMEM)
    return pl.pallas_call(
        shares_kernel,
        in_specs=[pl.BlockSpec(memory_space=pltpu.SMEM), vmem, ANYWHERE],
        out_specs=[vmem] * 4,
        out_shape=[
            shape_of(48, FF),
            shape_of(192, D),
            shape_of(96, D, dtype=bf16),
            shape_of(96, D, dtype=bf16),
        ],
        compiler_params=pltpu.CompilerParams(vmem_limit_bytes=32 * MIB),
        cost_estimate=lasting(3),
        name="shares",
    )(place, big, before)


def finish_kernel(
    total_ref,
    rest_ref,
    in_ref,
    gain_ref,
    before_ref,
    grad_in_ref,
    out_ref,
    norm_ref,
    state_ref,
    step_ref,
    decay_ref,
    conv_ref,
    conv_bias_ref,
    step_bias_ref,
    skip_ref,
    moe_ref,
    router_ref,
):
    total = jnp.sum(total_ref[...].astype(f32), axis=0)
    rest = rest_ref[...].astype(f32)
    out_ref[...] = rest[:12]
    grad_in_ref[:, :DI] = total[:6]
    grad_in_ref[:, DI : DI + D] = rest[12:18]
    grad_in_ref[:, DI + D :] = rest[18:24]
    part = jnp.sum(in_ref[...].astype(f32) * grad_in_ref[...], axis=1, keepdims=True)
    part = jnp.concatenate([jnp.broadcast_to(part, (6, LANES)), jnp.zeros((2, LANES), f32)], axis=0)
    norm_ref[...] = part.T[:1, :6] / gain_ref[...].astype(f32)
    rows = jnp.concatenate(
        [total[6 + c // 6 : 7 + c // 6, c % 6 * 160 : c % 6 * 160 + 160] for c in range(12)]
        + [jnp.zeros((4, 160), f32)],
        axis=0,
    )
    state_ref[...] = rows[:12, 72:152]
    turned = rows.T[:, :12]
    step_ref[...] = turned[:48]
    decay_ref[...] = turned[48:64]
    step_bias_ref[...] = turned[64:65]
    conv_ref[...] = turned[152:156]
    conv_bias_ref[...] = turned[156:157]
    skip_ref[...] = turned[157:158]
    wide = jnp.concatenate(
        [total[6:7, 960 + 16 * c : 976 + 16 * c] for c in range(6)] + [jnp.zeros((2, 16), f32)], axis=0
    )
    router_ref[...] = wide[:6, 1:9]
    moe_ref[...] = wide.T[:1, :6]


def finish_call(total, rest, in_proj, gain, before):
    return pl.pallas_call(
        finish_kernel,
        in_specs=[pl.BlockSpec(memory_space=pltpu.VMEM)] * 4 + [ANYWHERE],
        out_shape=[
            shape_of(6, 2 * DI),
            shape_of(12, D),
            shape_of(1, 6),
            shape_of(12, 80),
            shape_of(RANK, 12),
            shape_of(STATE, 12),
            shape_of(CONV, 12),
            shape_of(1, 12),
            shape_of(1, 12),
            shape_of(1, 12),
            shape_of(1, 6),
            shape_of(6, EXPERTS),
        ],
        compiler_params=pltpu.CompilerParams(vmem_limit_bytes=32 * MIB),
        cost_estimate=lasting(3),
        name="finish",
    )(total, rest, in_proj, gain, before)


def swap(v, axis):
    return lax.all_to_all(v, axis, 0, 0, tiled=True)


def spread(v, axis):
    n = lax.axis_size(axis) if isinstance(axis, str) else 128
    return swap(jnp.broadcast_to(v[None], (n,) + v.shape), axis)


def tied(*values):
    return lax.optimization_barrier(values)


CORE_SWAP = [(i, i ^ 1) for i in range(8)]
HOPS = (1, -1, 2)


def along_z(v, by):
    return lax.ppermute(
        v, "fsdp", [(2 * z + c, 2 * ((z + by) % CHIPS) + c) for z in range(CHIPS) for c in range(2)]
    )


def cores_total(own, other):
    return (own.astype(f32) + lax.ppermute(other, "fsdp", CORE_SWAP).astype(f32)).astype(bf16)


def chips_total(parts):
    parts = parts.reshape(CHIPS, parts.shape[0] // CHIPS, parts.shape[1])
    parts = [parts[0]] + [along_z(parts[i + 1], -by) for i, by in enumerate(HOPS)]
    return sum(p.astype(f32) for p in parts).astype(bf16)


def on_device(
    block_input,
    routes,
    cotangent,
    in_proj,
    conv_weight,
    conv_bias,
    state_proj,
    step_proj,
    step_bias,
    decay_log,
    skip_gain,
    out_proj,
    norm_gain,
    moe_gain,
    router,
    expert_up,
    expert_down,
):
    T = TOK
    place = lax.axis_index("fsdp").astype(jnp.int32)
    place = jnp.stack([place // 2, place % 2])
    small = jnp.concatenate(
        [
            state_proj,
            step_proj.T,
            decay_log.T,
            conv_weight.T,
            conv_bias[:, None],
            step_bias[:, None],
            skip_gain[:, None],
            jnp.zeros((12, 1), bf16),
        ],
        axis=1,
    ).reshape(1, 12 * WEIGHT_ROWS)
    wide = jnp.concatenate([norm_gain[:, None], moe_gain[:, None], router], axis=1)
    packed = jnp.concatenate([small, wide.reshape(1, 60), jnp.zeros((1, 1188), bf16)], axis=1)
    rows_c = spread(in_proj[:, :DI], "seq").reshape(96, DI)
    rows_late = jnp.concatenate(
        [in_proj[:, DI : DI + D], out_proj[:6], in_proj[:, DI + D :], out_proj[6:]], axis=1
    )
    rows_late = jnp.concatenate([rows_late, packed, jnp.zeros((1, 2 * DI), bf16)], axis=0)
    rows_c, rows_late = tied(rows_c, rows_late)
    in_c = lax.all_gather(rows_c, "fsdp", axis=0, tiled=True)
    rows_late = spread(rows_late, "seq")
    packed = swap(jnp.broadcast_to(rows_late[None, :, 6, :2048], (8, 16, 2048)), "fsdp")
    packed = packed.transpose(1, 0, 2).reshape(DEVICES, 2048)
    late = lax.all_gather(rows_late[:, :6].reshape(96, 2 * DI), "fsdp", axis=0, tiled=True)
    up_rows = expert_up[0].reshape(48, NFB, FB).transpose(1, 0, 2).reshape(192, FB)
    big = jnp.concatenate([up_rows, expert_down[0]], axis=0)

    weights = packed[:, : 12 * WEIGHT_ROWS].reshape(DI, WEIGHT_ROWS).T
    wide = packed[:, 12 * WEIGHT_ROWS : 12 * WEIGHT_ROWS + 60].reshape(D, 10).T
    norm_g, moe_g, router_w = wide[0:1].astype(f32), wide[1:2].astype(f32), wide[2:]

    x_tail = lax.ppermute(block_input[:, T - CONV + 1 :], ALL, [(i, i + 1) for i in range(127)])
    x_head = jnp.concatenate(
        [jnp.zeros((MICRO, HEAD - CONV + 1, D), bf16), x_tail, block_input], axis=1
    )
    normed_nat, normed_in, conv_in, conv, state_in, step_low, step, sig = front_call(
        x_head, norm_g, in_c, weights
    )
    conv_in, big = tied(conv_in, big)
    big = lax.all_gather(big, "seq", axis=0, tiled=False)
    x = block_input.reshape(MICRO * T, D).astype(f32)
    in_map = jnp.broadcast_to(
        state_in[:, :, RANK : RANK + STATE, None], (MICRO, T, STATE, LANES)
    )
    ends = end_state(step, conv, in_map, weights)
    pair = swap(ends, ALL)
    gate_act, gate_slope, out_w = gate_call(normed_in, late, ends)
    start = prefix(pair, pair, False, out_w)
    out_map = rows_call(RANK + STATE, state_in, start)
    start = swap(start, ALL)
    one_hot_i = (
        routes.reshape(MICRO, T, 1) == lax.broadcasted_iota(jnp.int32, (MICRO, T, EXPERTS), 2)
    ).astype(jnp.int32)
    slot = jnp.sum((jnp.cumsum(one_hot_i, axis=1) - 1) * one_hot_i, axis=2)
    micro = lax.broadcasted_iota(jnp.int32, (MICRO, T), 0)
    position = (routes.reshape(MICRO, T) * (MICRO * CAP) + micro * CAP + slot).reshape(
        1, MICRO * T
    )
    table = (lax.broadcasted_iota(jnp.int32, (ROWS, MICRO * T), 0) == position).astype(bf16)
    one_hot = one_hot_i.reshape(MICRO * T, EXPERTS).astype(f32)
    grad_out = cotangent.reshape(MICRO * T, D).astype(f32)

    mixed_y, gated = scan(step, conv, in_map, out_map, weights, start, gate_act.reshape(MICRO, T, DI))
    gated = gated.reshape(MICRO * T, DI)
    residual, expert_gate, probs, sent = dispatch_call(
        gated,
        out_w,
        block_input.reshape(MICRO * T, D),
        moe_g,
        router_w,
        one_hot,
        table,
        cotangent.reshape(MICRO * T, D),
    )
    ah = history(step, conv, in_map, weights, start, sent)
    sent = swap(sent, "fsdp")
    hidden, grad_pre, back = expert_call(sent, big, ah)
    back = swap(back, "fsdp")
    grad_experts = expert_grad_call(sent, hidden, grad_pre)
    mixed, grad_residual, grad_mix, grad_y, grad_gate_branch, wide = combine_call(
        table,
        back,
        residual,
        expert_gate,
        probs,
        one_hot,
        cotangent.reshape(MICRO * T, D),
        router_w,
        moe_g,
        out_w,
        gate_act,
        gate_slope,
        mixed_y.reshape(MICRO * T, DI),
        grad_experts,
    )
    grad_y = grad_y.reshape(MICRO, T, DI)
    mu = end_adjoint(step, grad_y, out_map, weights)
    mus = swap(mu, ALL)
    grad_big = early_grad_call(grad_experts, gated, grad_mix, normed_nat, grad_gate_branch, grad_mix)
    grad_early = grad_big
    grad_big = lax.psum_scatter(
        grad_big.reshape(16 * 576, D), "seq", scatter_dimension=0, tiled=True
    )
    later = swap(prefix(pair, mus, True, grad_early), ALL)
    wide = wide.astype(bf16).T.reshape(DEVICES, 1, 96)

    grad_first, grad_cin, grad_halo, grad_second = scan_back(
        step, sig, conv, grad_y, ah, in_map, out_map, weights, later, conv_in, step_low, state_in
    )
    grad_next = lax.ppermute(grad_halo, ALL, [(i + 1, i) for i in range(127)])
    smalls = jnp.concatenate(
        [grad_first[0] + grad_first[1], grad_second[0] + grad_second[1]], axis=0
    ).astype(bf16)
    smalls = smalls.T.reshape(DEVICES, 2, 960)
    wide = jnp.pad(wide, ((0, 0), (0, 1), (0, 480)))
    smalls = jnp.concatenate([smalls, wide], axis=2).reshape(2 * DEVICES, DI)
    grad_cin, other = other_grad_call(place, grad_cin, grad_next, normed_nat, smalls)
    total = cores_total(own_grad_call(place, grad_cin, normed_nat, smalls), other)
    operand = total
    total = lax.all_to_all(
        total.reshape(64, 8, DI),
        ALL,
        0,
        0,
        tiled=True,
        axis_index_groups=[list(range(c, DEVICES, 2)) for c in (0, 1)],
    )
    grad_input = input_grad_call(
        grad_cin, grad_gate_branch, in_c, late, x, norm_g, grad_residual, operand
    )
    grad_up, grad_down, own, other = shares_call(place, grad_big, grad_input)
    rest = chips_total(cores_total(own, other))
    (
        grad_in,
        grad_out_proj,
        grad_norm,
        grad_state,
        grad_step,
        grad_decay,
        grad_conv_weight,
        grad_conv_bias,
        grad_step_bias,
        grad_skip,
        grad_moe,
        grad_router,
    ) = finish_call(total, rest, in_proj, norm_gain.reshape(1, 6), grad_input)
    return (
        mixed.reshape(MICRO, T, D),
        grad_input.reshape(MICRO, T, D),
        grad_in,
        grad_conv_weight,
        grad_conv_bias.reshape(12),
        grad_state,
        grad_step,
        grad_step_bias.reshape(12),
        grad_decay,
        grad_skip.reshape(12),
        grad_out_proj,
        grad_norm.reshape(6),
        grad_moe.reshape(6),
        grad_router,
        grad_up[None],
        grad_down[None],
    )


def solution(mesh):
    return jax.shard_map(
        on_device,
        mesh=mesh,
        in_specs=(
            P(None, ALL, None),
            P(None, ALL, None),
            P(None, ALL, None),
            P(ALL, None),
            P(None, ALL),
            P(ALL),
            P(ALL, None),
            P(None, ALL),
            P(ALL),
            P(None, ALL),
            P(ALL),
            P(ALL, None),
            P(ALL),
            P(ALL),
            P(ALL, None),
            P("fsdp", "seq", None),
            P("fsdp", "seq", None),
        ),
        out_specs=(
            P(None, ALL, None),
            P(None, ALL, None),
            P(ALL, None),
            P(None, ALL),
            P(ALL),
            P(ALL, None),
            P(None, ALL),
            P(ALL),
            P(None, ALL),
            P(ALL),
            P(ALL, None),
            P(ALL),
            P(ALL),
            P(ALL, None),
            P("fsdp", "seq", None),
            P("fsdp", "seq", None),
        ),
        check_vma=False,
    )
```

```python
from functools import partial

import jax
import jax.numpy as jnp
from jax import lax
from jax.experimental import pallas as pl
from jax.experimental.pallas import tpu as pltpu
from jax.sharding import PartitionSpec as P

D = 768
DI = 1536
STATE = 16
RANK = 48
CONV = 4
FF = 3072
TOK = 128
MICRO = 2
EXPERTS = 8
DEVICES = 128
CHIPS = 4
WEIGHT_ROWS = 152
CAP = 20
LANES = 128
CB = 768
NCB = DI // CB
SUB = 384
SUBS = CB // SUB
TILES = SUB // LANES
HEAD = 8
ALL = ("seq", "fsdp")
EPSILON = 1e-05
LOG2E = 1.4426950408889634
LN2 = 0.6931471805599453
MIB = 1024 * 1024
HIGHEST = lax.Precision.HIGHEST
bf16 = jnp.bfloat16
f32 = jnp.float32


def dot(a, b, ca, cb, precision=None):
    return lax.dot_general(
        a, b, (((ca,), (cb,)), ((), ())), precision=precision, preferred_element_type=f32
    )


def silu_parts(v):
    s = jax.nn.sigmoid(v)
    return v * s, s * (1.0 + v * (1.0 - s))


def tile_of(j):
    return slice(j * LANES, (j + 1) * LANES)


class Fold:
    def __init__(self, falling=False):
        self.held = []
        self.falling = falling

    def add(self, part):
        part, level = part[:8] + part[8:], 0
        while self.held and self.held[-1][1] == level:
            other = self.held.pop()[0]
            a, b = (part, other) if self.falling else (other, part)
            d = 1 << level
            low = (lax.broadcasted_iota(jnp.int32, (8, LANES), 0) & d) == 0
            part = jnp.where(low, a, b) + pltpu.roll(jnp.where(low, b, a), 8 - d, 0)
            level += 1
        self.held.append((part, level))

    def result(self):
        return self.held[0][0]


def load_decay(weights_ref):
    rows = weights_ref[128:144, :].astype(f32)
    return [(-LOG2E) * jnp.exp(rows[:, tile_of(j)]) for j in range(SUBS * TILES)]


def tiles_of(sub):
    return range(sub * TILES, (sub + 1) * TILES)


def load_state(ref, sub):
    state = ref[sub * STATE : (sub + 1) * STATE].reshape(STATE, SUB)
    return tuple(state[:, tile_of(j)] for j in range(TILES))


def aligned(tb):
    return pl.ds(pl.multiple_of(tb * 8, 8), 8)


ZERO_STATE = (STATE, LANES)


def spread_map(state_ref, first, out_ref):
    @pl.when(pl.program_id(1) == 0)
    def _():
        part = state_ref[0][:, first : first + STATE]
        out_ref[...] = jnp.broadcast_to(part[:, :, None], (TOK, STATE, LANES))


def end_state_kernel(step_ref, conv_ref, state_ref, weights_ref, out_ref, b_ref):
    spread_map(state_ref, RANK, b_ref)
    decay = load_decay(weights_ref)

    def block(sub, tb, hs):
        hs = list(hs)
        columns = slice(sub * SUB, (sub + 1) * SUB)
        dt8 = step_ref[0, aligned(tb), columns]
        u8 = dt8 * conv_ref[0, aligned(tb), columns]
        for i in range(8):
            b = b_ref[tb * 8 + i]
            for j in range(TILES):
                dt = dt8[i : i + 1, tile_of(j)]
                u = u8[i : i + 1, tile_of(j)]
                hs[j] = jnp.exp2(dt * decay[sub * TILES + j]) * hs[j] + b * u
        return tuple(hs)

    zero = jnp.zeros(ZERO_STATE, f32)
    total = jnp.sum(step_ref[0], axis=0, keepdims=True)
    for sub in range(SUBS):
        hs = lax.fori_loop(0, TOK // 8, partial(block, sub), (zero,) * TILES)
        rows = slice(sub * STATE, (sub + 1) * STATE)
        for j in range(TILES):
            k = sub * TILES + j
            prod = jnp.exp2(total[:, tile_of(k)] * decay[k])
            out_ref[rows, :, tile_of(j)] = prod.reshape(STATE, 1, LANES)
            out_ref[rows, :, tile_of(j + TILES)] = hs[j].reshape(STATE, 1, LANES)


def scan_kernel(
    step_ref, conv_ref, state_ref, weights_ref, start_ref, act_ref, my_ref, gated_ref, b_ref, c_ref
):
    spread_map(state_ref, RANK, b_ref)
    spread_map(state_ref, RANK + STATE, c_ref)
    decay = load_decay(weights_ref)
    skip = weights_ref[144:152, :].astype(f32)[6:7]

    def block(sub, tb, hs):
        hs = list(hs)
        columns = slice(sub * SUB, (sub + 1) * SUB)
        dt8 = step_ref[0, aligned(tb), columns]
        conv8 = conv_ref[0, aligned(tb), columns]
        u8 = dt8 * conv8
        outs = [Fold() for _ in range(TILES)]
        for i in range(8):
            t = tb * 8 + i
            b = b_ref[t]
            c = c_ref[t]
            for j in range(TILES):
                dt = dt8[i : i + 1, tile_of(j)]
                u = u8[i : i + 1, tile_of(j)]
                hs[j] = jnp.exp2(dt * decay[sub * TILES + j]) * hs[j] + b * u
                outs[j].add(hs[j] * c)
        for j in range(TILES):
            k = sub * TILES + j
            my_ref[0, aligned(tb), tile_of(k)] = (
                outs[j].result() + skip[:, tile_of(k)] * conv8[:, tile_of(j)]
            )
        return tuple(hs)

    for sub in range(SUBS):
        lax.fori_loop(0, TOK // 8, partial(block, sub), load_state(start_ref, sub))
    gated_ref[0] = (my_ref[0] * act_ref[0]).astype(bf16)


def history_kernel(step_ref, conv_ref, state_ref, weights_ref, start_ref, before_ref, ah_ref, b_ref):
    spread_map(state_ref, RANK, b_ref)
    decay = load_decay(weights_ref)

    def block(sub, tb, hs):
        hs = list(hs)
        columns = slice(sub * SUB, (sub + 1) * SUB)
        dt8 = step_ref[0, aligned(tb), columns]
        u8 = dt8 * conv_ref[0, aligned(tb), columns]
        for i in range(8):
            t = tb * 8 + i
            b = b_ref[t]
            for j in range(TILES):
                dt = dt8[i : i + 1, tile_of(j)]
                u = u8[i : i + 1, tile_of(j)]
                ah = jnp.exp2(dt * decay[sub * TILES + j]) * hs[j]
                ah_ref[0, t, :, tile_of(sub * TILES + j)] = ah.astype(bf16)
                hs[j] = ah + b * u
        return tuple(hs)

    for sub in range(SUBS):
        lax.fori_loop(0, TOK // 8, partial(block, sub), load_state(start_ref, sub))


def end_adjoint_kernel(step_ref, gy_ref, state_ref, weights_ref, mu_ref, c_ref):
    spread_map(state_ref, RANK + STATE, c_ref)
    decay = load_decay(weights_ref)

    def block(sub, k, mus):
        mus = list(mus)
        columns = slice(sub * SUB, (sub + 1) * SUB)
        tb = TOK // 8 - 1 - k
        dt8 = step_ref[0, aligned(tb), columns]
        gy8 = gy_ref[0, aligned(tb), columns]
        for i in reversed(range(8)):
            c = c_ref[tb * 8 + i]
            for j in range(TILES):
                dt = dt8[i : i + 1, tile_of(j)]
                gy = gy8[i : i + 1, tile_of(j)]
                mus[j] = jnp.exp2(dt * decay[sub * TILES + j]) * (mus[j] + c * gy)
        return tuple(mus)

    zero = jnp.zeros(ZERO_STATE, f32)
    for sub in range(SUBS):
        mus = lax.fori_loop(0, TOK // 8, partial(block, sub), (zero,) * TILES)
        for j in range(TILES):
            mu_ref[sub * STATE : (sub + 1) * STATE, :, tile_of(j)] = mus[j].reshape(STATE, 1, LANES)


def scan_back_kernel(
    step_ref,
    sig_ref,
    conv_ref,
    gy_ref,
    ah_ref,
    state_ref,
    weights_ref,
    all_ref,
    later_ref,
    cin_ref,
    low_ref,
    first_ref,
    gcin_ref,
    halo_ref,
    second_ref,
    glow_ref,
    guy_ref,
    s1_ref,
    s2_ref,
    gb_ref,
    gc_ref,
    b_ref,
    c_ref,
    conv_low_ref,
):
    phase = pl.program_id(1)
    spread_map(state_ref, RANK, b_ref)
    spread_map(state_ref, RANK + STATE, c_ref)

    @pl.when(phase == 0)
    def _():
        gb_ref[...] = jnp.zeros_like(gb_ref)
        gc_ref[...] = jnp.zeros_like(gc_ref)
        glow_ref[...] = jnp.zeros_like(glow_ref)
        guy_ref[...] = jnp.zeros_like(guy_ref)

    @pl.when(phase < NCB)
    def _():
        decay = load_decay(weights_ref)

        def backward(sub, k, carry):
            mus, gds = list(carry[0]), list(carry[1])
            columns = slice(sub * SUB, (sub + 1) * SUB)
            tb = TOK // 8 - 1 - k
            dt8 = step_ref[0, aligned(tb), columns]
            u8 = dt8 * conv_ref[0, aligned(tb), columns]
            gy8 = gy_ref[0, aligned(tb), columns]
            out1 = [Fold(True) for _ in range(TILES)]
            out2 = [Fold(True) for _ in range(TILES)]
            for i in reversed(range(8)):
                t = tb * 8 + i
                b = b_ref[t]
                c = c_ref[t]
                gb = gb_ref[t]
                gc = gc_ref[t]
                for j in range(TILES):
                    dt = dt8[i : i + 1, tile_of(j)]
                    u = u8[i : i + 1, tile_of(j)]
                    gy = gy8[i : i + 1, tile_of(j)]
                    ah = ah_ref[0, t, :, tile_of(sub * TILES + j)].astype(f32)
                    z = dt * decay[sub * TILES + j]
                    lam = c * gy + mus[j]
                    w = lam * ah * z
                    out1[j].add(lam * b)
                    out2[j].add(w)
                    gds[j] = gds[j] + w
                    gb = gb + lam * u
                    gc = gc + gy * ah
                    mus[j] = jnp.exp2(z) * lam
                gb_ref[t] = gb
                gc_ref[t] = gc
            for j in range(TILES):
                k = sub * TILES + j
                s1_ref[phase, aligned(tb), tile_of(k)] = out1[j].result()
                s2_ref[aligned(tb), tile_of(k)] = out2[j].result()
            return tuple(mus), tuple(gds)

        zero = jnp.zeros(ZERO_STATE, f32)
        for sub in range(SUBS):
            _, gds = lax.fori_loop(
                0,
                TOK // 8,
                partial(backward, sub),
                (load_state(later_ref, sub), (zero,) * TILES),
            )
            for j in range(TILES):
                first_ref[0, 48:64, tile_of(sub * TILES + j)] = LN2 * gds[j]
        step, conv, sig, gy, s1 = step_ref[0], conv_ref[0], sig_ref[0], gy_ref[0], s1_ref[phase]
        share = jnp.where(step > 1e-30, sig / jnp.maximum(step, 1e-30), 1.0)
        gsp = LN2 * s2_ref[...] * share + conv * s1 * sig
        guy_ref[...] += jnp.sum(gy * step * conv, axis=1, keepdims=True)
        s1_ref[phase] = step * s1 + weights_ref[144:152, :].astype(f32)[6:7] * gy
        conv_low_ref[phase] = conv.astype(bf16)
        gsp_low = gsp.astype(bf16)
        first_ref[0, 0:48, :] = dot(low_ref[0], gsp_low, 0, 0)
        first_ref[0, 64:65, :] = jnp.sum(gsp, axis=0, keepdims=True)
        first_ref[0, 65:66, :] = jnp.sum(gy * conv, axis=0, keepdims=True)
        first_ref[0, 66:72, :] = jnp.zeros((6, CB), f32)
        glow_ref[:, 0:48] += dot(gsp_low, weights_ref[80:128, :], 1, 1)

    @pl.when(phase == NCB)
    def _():
        glow_ref[:, 48:64] = jnp.sum(gb_ref[...], axis=-1)
        glow_ref[:, 64:80] = jnp.sum(gc_ref[...], axis=-1) + guy_ref[...] * state_ref[0][:, 48:64]

    @pl.when(phase == NCB)
    def _():
        glow = glow_ref[...].astype(bf16)
        for block in range(NCB):
            columns = slice(block * CB, (block + 1) * CB)
            vecs = all_ref[144:152, columns].astype(f32)
            gconv = s1_ref[block] + dot(glow, all_ref[0:80, columns], 1, 0)
            second_ref[0, 0:80, columns] = dot(glow, conv_low_ref[block], 0, 0)
            cin = cin_ref[0, :, columns].astype(f32)
            first = HEAD - CONV + 1
            pieces = [cin[first + i : first + i + TOK] for i in range(CONV)]
            v = vecs[4:5] + sum(vecs[i : i + 1] * pieces[i] for i in range(CONV))
            gv = gconv * silu_parts(v)[1]
            for i in range(CONV):
                second_ref[0, 80 + i : 81 + i, columns] = jnp.sum(
                    gv * pieces[i], axis=0, keepdims=True
                )
            second_ref[0, 84:85, columns] = jnp.sum(gv, axis=0, keepdims=True)
            second_ref[0, 85:88, columns] = jnp.zeros((3, CB), f32)
            edge = jnp.zeros((8, CB), f32)
            padded = jnp.concatenate([edge, gv, edge], axis=0)
            gcin = sum(
                vecs[i : i + 1] * padded[CONV - 1 - i : CONV - 1 - i + TOK + HEAD]
                for i in range(CONV)
            )
            halo_ref[0, :, columns] = gcin[:HEAD]
            gcin_ref[0, :, columns] = gcin[HEAD:]


def same(c):
    return c


def at(c):
    return jnp.minimum(c, NCB - 1)


def wrap(c):
    return lax.rem(c, NCB)


def second(c):
    return jnp.maximum(c - NCB, 0)


def token_spec(place=same, rows=TOK):
    return pl.BlockSpec((1, rows, CB), lambda m, c: (m, 0, place(c)))


def weights_spec(place=same):
    return pl.BlockSpec((WEIGHT_ROWS, CB), lambda m, c: (0, place(c)))


ANYWHERE = pl.BlockSpec(memory_space=pl.ANY)
STATE_INPUTS = pl.BlockSpec((1, TOK, 80), lambda m, c: (m, 0, 0))
MAP = pltpu.VMEM((TOK, STATE, LANES), f32)


def state_spec(width=SUB, place=same):
    return pl.BlockSpec((SUBS * STATE, 1, width), lambda m, c: (m * NCB + place(c), 0, 0))


def history_spec(place=same):
    return pl.BlockSpec((1, TOK, STATE, CB), lambda m, c: (m, 0, 0, place(c)))


def shape_of(*shape, dtype=f32):
    return jax.ShapeDtypeStruct(shape, dtype)


PARAMS = pltpu.CompilerParams(
    dimension_semantics=("arbitrary", "arbitrary"), vmem_limit_bytes=48 * MIB
)


def lasting(us):
    return pl.CostEstimate(flops=us * 10**9, bytes_accessed=us * 3 * 10**6, transcendentals=0)


def end_state(step, conv, state, weights):
    return pl.pallas_call(
        end_state_kernel,
        grid=(MICRO, NCB),
        in_specs=[token_spec(), token_spec(), STATE_INPUTS, weights_spec()],
        out_specs=state_spec(2 * SUB),
        out_shape=shape_of(DEVICES, 1, 2 * SUB),
        scratch_shapes=[MAP],
        compiler_params=PARAMS,
        cost_estimate=lasting(6),
        name="end_state",
    )(step, conv, state, weights)


def scan(step, conv, state, weights, start, act):
    return pl.pallas_call(
        scan_kernel,
        grid=(MICRO, NCB),
        in_specs=[
            token_spec(),
            token_spec(),
            STATE_INPUTS,
            weights_spec(),
            state_spec(),
            token_spec(),
        ],
        out_specs=[token_spec(), token_spec()],
        out_shape=[shape_of(MICRO, TOK, DI), shape_of(MICRO, TOK, DI, dtype=bf16)],
        scratch_shapes=[MAP, MAP],
        compiler_params=PARAMS,
        cost_estimate=lasting(12),
        name="scan",
    )(step, conv, state, weights, start, act)


def history(step, conv, state, weights, start, before):
    return pl.pallas_call(
        history_kernel,
        grid=(MICRO, NCB),
        in_specs=[token_spec(), token_spec(), STATE_INPUTS, weights_spec(), state_spec(), ANYWHERE],
        out_specs=history_spec(),
        out_shape=shape_of(MICRO, TOK, STATE, DI, dtype=bf16),
        scratch_shapes=[MAP],
        compiler_params=PARAMS,
        cost_estimate=lasting(12),
        name="history",
    )(step, conv, state, weights, start, before)


def end_adjoint(step, gy, state, weights):
    return pl.pallas_call(
        end_adjoint_kernel,
        grid=(MICRO, NCB),
        in_specs=[token_spec(), token_spec(), STATE_INPUTS, weights_spec()],
        out_specs=state_spec(),
        out_shape=shape_of(DEVICES, 1, SUB),
        scratch_shapes=[MAP],
        compiler_params=PARAMS,
        cost_estimate=lasting(6),
        name="end_adjoint",
    )(step, gy, state, weights)


def scan_back(step, sig, conv, gy, ah, state, weights, later, cin, low):
    return pl.pallas_call(
        scan_back_kernel,
        grid=(MICRO, NCB + 1),
        in_specs=[
            token_spec(at),
            token_spec(at),
            token_spec(at),
            token_spec(at),
            history_spec(at),
            STATE_INPUTS,
            weights_spec(at),
            pl.BlockSpec((WEIGHT_ROWS, DI), lambda m, c: (0, 0)),
            state_spec(SUB, at),
            pl.BlockSpec((1, TOK + HEAD, DI), lambda m, c: (m, 0, 0)),
            pl.BlockSpec((1, TOK, RANK), lambda m, c: (m, 0, 0)),
        ],
        out_specs=[
            token_spec(at, 72),
            pl.BlockSpec((1, TOK, DI), lambda m, c: (m, 0, 0)),
            pl.BlockSpec((1, HEAD, DI), lambda m, c: (m, 0, 0)),
            pl.BlockSpec((1, 88, DI), lambda m, c: (m, 0, 0)),
        ],
        out_shape=[
            shape_of(MICRO, 72, DI),
            shape_of(MICRO, TOK, DI),
            shape_of(MICRO, HEAD, DI),
            shape_of(MICRO, 88, DI),
        ],
        scratch_shapes=[
            pltpu.VMEM((TOK, 80), f32),
            pltpu.VMEM((TOK, 1), f32),
            pltpu.VMEM((NCB, TOK, CB), f32),
            pltpu.VMEM((TOK, CB), f32),
            MAP,
            MAP,
            MAP,
            MAP,
            pltpu.VMEM((NCB, TOK, CB), bf16),
        ],
        compiler_params=PARAMS,
        cost_estimate=lasting(36),
        name="scan_back",
    )(step, sig, conv, gy, ah, state, weights, weights, later, cin, low)


def prefix_kernel(reverse, prod_ref, state_ref, before_ref, out_ref):
    skipped = state_ref.shape[2] - SUB

    def one(k, state):
        i = DEVICES - 1 - k if reverse else k
        out_ref[i] = state
        return prod_ref[i, :, :SUB] * state + state_ref[i, :, skipped:]

    lax.fori_loop(0, DEVICES, one, jnp.zeros((1, SUB), f32), unroll=8)


def prefix(prod, state, reverse, before):
    return pl.pallas_call(
        partial(prefix_kernel, reverse),
        in_specs=[pl.BlockSpec(memory_space=pltpu.VMEM)] * 2 + [ANYWHERE],
        out_shape=shape_of(DEVICES, 1, SUB),
        cost_estimate=lasting(2),
        name="prefix",
    )(prod, state, before)


ROWS = EXPERTS * MICRO * CAP
FB = 768
NFB = FF // FB
EXP_PARAMS = pltpu.CompilerParams(
    dimension_semantics=("arbitrary",), vmem_limit_bytes=56 * MIB
)


def gelu_parts(v):
    c = 0.7978845608028654
    v2 = v * v
    th = jnp.tanh(c * (v + 0.044715 * v * v2))
    half = 0.5 * (1.0 + th)
    return v * half, half + 0.5 * v * (1.0 - th * th) * c * (1.0 + 3 * 0.044715 * v2)


def expert_kernel(rows_ref, up_ref, down_ref, before_ref, hidden_ref, gpre_ref, out_ref, acc_ref):
    j = pl.program_id(0)
    up = up_ref[...].reshape(D, FB)
    down = down_ref[...].reshape(FB, D)
    x = rows_ref[:, :D]
    g = rows_ref[:, D:]
    act, slope = gelu_parts(dot(x, up, 1, 0))
    hidden = act.astype(bf16)
    gpre = (dot(g, down, 1, 1) * slope).astype(bf16)
    hidden_ref[...] = hidden
    gpre_ref[...] = gpre
    eo = dot(hidden, down, 1, 0)
    gr = dot(gpre, up, 1, 1)

    @pl.when(j == 0)
    def _():
        acc_ref[:, :D] = eo
        acc_ref[:, D:] = gr

    @pl.when(j > 0)
    def _():
        acc_ref[:, :D] += eo
        acc_ref[:, D:] += gr

    @pl.when(j == NFB - 1)
    def _():
        out_ref[...] = acc_ref[...].astype(bf16)


def expert_call(rows, weights, before):
    return pl.pallas_call(
        expert_kernel,
        grid=(NFB,),
        in_specs=[
            pl.BlockSpec((ROWS, 2 * D), lambda j: (0, 0)),
            pl.BlockSpec((16, 48, D), lambda j: (0, j, 0)),
            pl.BlockSpec((4, 192, D), lambda j: (j, 1, 0)),
            ANYWHERE,
        ],
        out_specs=[
            pl.BlockSpec((ROWS, FB), lambda j: (0, j)),
            pl.BlockSpec((ROWS, FB), lambda j: (0, j)),
            pl.BlockSpec((ROWS, 2 * D), lambda j: (0, 0)),
        ],
        out_shape=[
            jax.ShapeDtypeStruct((ROWS, FF), bf16),
            jax.ShapeDtypeStruct((ROWS, FF), bf16),
            jax.ShapeDtypeStruct((ROWS, 2 * D), bf16),
        ],
        scratch_shapes=[pltpu.VMEM((ROWS, 2 * D), f32)],
        compiler_params=EXP_PARAMS,
        cost_estimate=lasting(11),
        name="expert",
    )(rows, weights, weights, before)


def expert_grad_kernel(rows_ref, hidden_ref, gpre_ref, out_ref):
    j = pl.program_id(0)
    gup = dot(rows_ref[:, :D], gpre_ref[...], 0, 0).astype(bf16)
    gdown = dot(hidden_ref[...], rows_ref[:, D:], 0, 0).astype(bf16)
    out_ref[:, pl.ds(pl.multiple_of(j * 48, 16), 48), :] = gup.reshape(16, 48, D)
    out_ref[pl.ds(j * 4, 4), 192:384, :] = gdown.reshape(4, 192, D)


def expert_grad_call(rows, hidden, gpre):
    return pl.pallas_call(
        expert_grad_kernel,
        grid=(NFB,),
        in_specs=[
            pl.BlockSpec((ROWS, 2 * D), lambda j: (0, 0)),
            pl.BlockSpec((ROWS, FB), lambda j: (0, j)),
            pl.BlockSpec((ROWS, FB), lambda j: (0, j)),
        ],
        out_specs=pl.BlockSpec((16, 384, D), lambda j: (0, 0, 0)),
        out_shape=shape_of(16, 576, D, dtype=bf16),
        compiler_params=EXP_PARAMS,
        cost_estimate=lasting(11),
        name="expert_grad",
    )(rows, hidden, gpre)


def picks(natural, size):
    shape = (size, natural.shape[1])
    return (lax.broadcasted_iota(jnp.int32, shape, 0) == natural).astype(bf16)


def split_dot(a, b):
    high = a.astype(bf16)
    low = (a - high.astype(f32)).astype(bf16)
    return dot(high, b, 1, 1) + dot(low, b, 1, 1)


def gathered_row(k, rows):
    return (k % (16 * rows) // rows * 8 + k // (16 * rows)) * rows + k % rows


def gate_kernel(normed_ref, late_ref, before_ref, act_ref, slope_ref, out_ref, total_ref):
    j = pl.program_id(0)
    act, slope = silu_parts(dot(normed_ref[...], late_ref[:, :D], 1, 0))
    act_ref[...] = act
    slope_ref[...] = slope
    k = lax.broadcasted_iota(jnp.int32, (1, D), 1)
    source = (k % 96 // 6 * 8 + k // 96) * 12 + j * 6 + k % 6
    part = dot(picks(source, DI), late_ref[:, D:], 1, 0)

    @pl.when(j == 0)
    def _():
        total_ref[...] = part

    @pl.when(j == 1)
    def _():
        out_ref[...] = (total_ref[...] + part).astype(bf16)


def gate_call(normed, late, before):
    return pl.pallas_call(
        gate_kernel,
        grid=(2,),
        in_specs=[
            pl.BlockSpec((MICRO * TOK, D), lambda j: (0, 0)),
            pl.BlockSpec((D, DI), lambda j: (0, j)),
            ANYWHERE,
        ],
        out_specs=[
            pl.BlockSpec((MICRO * TOK, D), lambda j: (0, j)),
            pl.BlockSpec((MICRO * TOK, D), lambda j: (0, j)),
            pl.BlockSpec((DI, D), lambda j: (0, 0)),
        ],
        out_shape=[
            shape_of(MICRO * TOK, DI),
            shape_of(MICRO * TOK, DI),
            shape_of(DI, D, dtype=bf16),
        ],
        scratch_shapes=[pltpu.VMEM((DI, D), f32)],
        compiler_params=EXP_PARAMS,
        cost_estimate=lasting(12),
        name="gate",
    )(normed, late, before)


def front_kernel(
    x_ref,
    gain_ref,
    in_c_ref,
    weights_ref,
    nat_ref,
    normed_ref,
    cin_ref,
    conv_ref,
    state_ref,
    low_ref,
    step_ref,
    sig_ref,
    rows_ref,
):
    phase = pl.program_id(0)

    @pl.when(phase == 0)
    def _():
        x = x_ref[...].astype(f32).reshape(MICRO * (TOK + HEAD), D)
        scale = lax.rsqrt(jnp.mean(x * x, axis=-1, keepdims=True) + EPSILON)
        nat = (x * scale * gain_ref[...]).astype(bf16)
        k = lax.broadcasted_iota(jnp.int32, (1, D), 1)
        rows_ref[...] = dot(nat, picks(gathered_row(k, 6), D), 1, 0).astype(bf16)
        for m in range(MICRO):
            first = m * (TOK + HEAD) + HEAD
            nat_ref[m * TOK : (m + 1) * TOK, :] = nat[first : first + TOK]
            normed_ref[m * TOK : (m + 1) * TOK, :] = rows_ref[first : first + TOK, :]
        state_ref[...] = jnp.zeros_like(state_ref)

    @pl.when(phase < NCB)
    def _():
        vecs = weights_ref[144:152, :].astype(f32)
        cin = dot(rows_ref[...], in_c_ref[...], 1, 0).astype(bf16).reshape(MICRO, TOK + HEAD, CB)
        cin_ref[...] = cin
        first = HEAD - CONV + 1
        for m in range(MICRO):
            rows = cin[m].astype(f32)
            v = vecs[4:5] + sum(
                vecs[i : i + 1] * rows[first + i : first + i + TOK] for i in range(CONV)
            )
            conv = silu_parts(v)[0].astype(bf16)
            conv_ref[m] = conv.astype(f32)
            state_ref[m] += dot(conv, weights_ref[0:80, :], 1, 1)

    @pl.when(phase == NCB)
    def _():
        low_ref[...] = state_ref[:, :, :RANK].astype(bf16)

    @pl.when(phase >= NCB)
    def _():
        bias = weights_ref[144:152, :].astype(f32)[5:6]
        for m in range(MICRO):
            pre = dot(low_ref[m], weights_ref[80:128, :], 1, 0) + bias
            step_ref[m] = jax.nn.softplus(pre)
            sig_ref[m] = jax.nn.sigmoid(pre)


def front_call(x, gain, in_c, weights):
    def blocks(rows, place):
        return pl.BlockSpec((MICRO, rows, CB), lambda c: (0, 0, place(c)))

    def whole(*shape):
        return pl.BlockSpec(shape, lambda c: (0,) * len(shape))

    return pl.pallas_call(
        front_kernel,
        grid=(2 * NCB,),
        in_specs=[
            whole(MICRO, TOK + HEAD, D),
            whole(1, D),
            pl.BlockSpec((D, CB), lambda c: (0, at(c))),
            pl.BlockSpec((WEIGHT_ROWS, CB), lambda c: (0, wrap(c))),
        ],
        out_specs=[
            whole(MICRO * TOK, D),
            whole(MICRO * TOK, D),
            blocks(TOK + HEAD, at),
            blocks(TOK, at),
            whole(MICRO, TOK, 80),
            whole(MICRO, TOK, RANK),
            blocks(TOK, second),
            blocks(TOK, second),
        ],
        out_shape=[
            shape_of(MICRO * TOK, D, dtype=bf16),
            shape_of(MICRO * TOK, D, dtype=bf16),
            shape_of(MICRO, TOK + HEAD, DI, dtype=bf16),
            shape_of(MICRO, TOK, DI),
            shape_of(MICRO, TOK, 80),
            shape_of(MICRO, TOK, RANK, dtype=bf16),
            shape_of(MICRO, TOK, DI),
            shape_of(MICRO, TOK, DI),
        ],
        scratch_shapes=[pltpu.VMEM((MICRO * (TOK + HEAD), D), bf16)],
        compiler_params=EXP_PARAMS,
        cost_estimate=lasting(8),
        name="front",
    )(x, gain, in_c, weights)


def owned_rows(core, normed, low_ref, small_ref, out_ref):
    k = lax.broadcasted_iota(jnp.int32, (1, 512), 1)
    row = k % 8
    inner = picks(jnp.where(row < 6, (k // 8 * 2 + core) * 6 + row, -1), D)
    inner = dot(normed, inner, 1, 0).astype(bf16)
    outer = picks(jnp.where(row < 6, -1, (k // 8 * 2 + core) * 2 + row - 6), 2 * DEVICES)
    for j in range(2):
        columns = slice(j * D, (j + 1) * D)
        part = dot(inner, low_ref[:, columns], 0, 0) + dot(outer, small_ref[:, columns], 0, 0)
        out_ref[:, columns] = part.astype(bf16)


def dispatch_kernel(
    gated_ref,
    out_w_ref,
    x_ref,
    gain_ref,
    router_ref,
    hot_ref,
    table_ref,
    grad_ref,
    residual_ref,
    gate_ref,
    probs_ref,
    sent_ref,
):
    part = dot(gated_ref[...], out_w_ref[...], 1, 0)

    @pl.when(pl.program_id(0) == 0)
    def _():
        residual_ref[...] = x_ref[...].astype(f32) + part

    @pl.when(pl.program_id(0) > 0)
    def _():
        residual_ref[...] += part

    @pl.when(pl.program_id(0) == NCB - 1)
    def _():
        residual = residual_ref[...]
        scale = lax.rsqrt(jnp.mean(residual * residual, axis=-1, keepdims=True) + EPSILON)
        normed = (residual * scale * gain_ref[...]).astype(bf16)
        logits = dot(normed, router_ref[...], 1, 1)
        powers = jnp.exp(logits - jnp.max(logits, axis=-1, keepdims=True))
        probs = powers / jnp.sum(powers, axis=-1, keepdims=True)
        gate = jnp.sum(probs * hot_ref[...], axis=-1, keepdims=True)
        probs_ref[...] = probs
        gate_ref[...] = gate
        sent_ref[:, :D] = dot(table_ref[...], normed, 1, 0).astype(bf16)
        grad = (gate * grad_ref[...].astype(f32)).astype(bf16)
        sent_ref[:, D:] = dot(table_ref[...], grad, 1, 0).astype(bf16)


def dispatch_call(gated, out_w, x, gain, router, hot, table, grad):
    tokens = MICRO * TOK

    def whole(*shape):
        return pl.BlockSpec(shape, lambda c: (0, 0))

    return pl.pallas_call(
        dispatch_kernel,
        grid=(NCB,),
        in_specs=[
            pl.BlockSpec((tokens, CB), lambda c: (0, c)),
            pl.BlockSpec((CB, D), lambda c: (c, 0)),
            whole(tokens, D),
            whole(1, D),
            whole(EXPERTS, D),
            whole(tokens, EXPERTS),
            whole(ROWS, tokens),
            whole(tokens, D),
        ],
        out_specs=[
            whole(tokens, D),
            whole(tokens, 1),
            whole(tokens, EXPERTS),
            whole(ROWS, 2 * D),
        ],
        out_shape=[
            shape_of(tokens, D),
            shape_of(tokens, 1),
            shape_of(tokens, EXPERTS),
            shape_of(ROWS, 2 * D, dtype=bf16),
        ],
        compiler_params=EXP_PARAMS,
        cost_estimate=lasting(4),
        name="dispatch",
    )(gated, out_w, x, gain, router, hot, table, grad)


def combine_kernel(
    table_ref,
    back_ref,
    residual_ref,
    gate_ref,
    probs_ref,
    hot_ref,
    grad_ref,
    router_ref,
    gain_ref,
    out_w_ref,
    act_ref,
    slope_ref,
    my_ref,
    gated_ref,
    normed_ref,
    held_ref,
    mixed_ref,
    grad_residual_ref,
    mix_ref,
    gy_ref,
    branch_ref,
    wide_ref,
    early_ref,
):
    @pl.when(pl.program_id(0) == 0)
    def _():
        returned = dot(table_ref[...], back_ref[...], 0, 0)
        expert_out, grad_in = returned[:, :D], returned[:, D:]
        residual, gate, grad = residual_ref[...], gate_ref[...], grad_ref[...].astype(f32)
        mixed_ref[...] = (residual + gate * expert_out).astype(bf16)
        grad_gate = jnp.sum(grad * expert_out, axis=-1, keepdims=True)
        grad_logits = grad_gate * gate * (hot_ref[...] - probs_ref[...])
        high = grad_logits.astype(bf16)
        low = (grad_logits - high.astype(f32)).astype(bf16)
        grad_in = grad_in + dot(high, router_ref[...], 1, 0) + dot(low, router_ref[...], 1, 0)
        scale = lax.rsqrt(jnp.mean(residual * residual, axis=-1, keepdims=True) + EPSILON)
        unit = residual * scale
        normed = (unit * gain_ref[...]).astype(bf16)
        wide_ref[0:1, :] = jnp.sum(grad_in * unit, axis=0, keepdims=True)
        wide_ref[1:9, :] = dot(high, normed, 0, 0) + dot(low, normed, 0, 0)
        wide_ref[9:16, :] = jnp.zeros((7, D), f32)
        scaled = grad_in * gain_ref[...]
        grad = grad + scale * (scaled - unit * jnp.mean(scaled * unit, axis=-1, keepdims=True))
        grad_residual_ref[...] = grad
        mix_ref[...] = grad.astype(bf16)
        part = dot(gated_ref[...], mix_ref[...], 0, 0)
        early_ref[:, 0:96, :] = part.astype(bf16).reshape(16, 96, D)

    grad = dot(mix_ref[...], out_w_ref[...], 1, 1)
    gy_ref[...] = grad * act_ref[...]
    branch_ref[...] = (grad * my_ref[...] * slope_ref[...]).astype(bf16)
    part = dot(normed_ref[...], branch_ref[...], 0, 0).astype(bf16).reshape(16, 48, D)
    early_ref[:, pl.ds(pl.multiple_of(96 + 48 * pl.program_id(0), 16), 48), :] = part


def combine_call(
    table, back, residual, gate, probs, hot, grad, router, gain, out_w, act, slope, my, gated, normed, held
):
    tokens = MICRO * TOK

    def whole(*shape):
        return pl.BlockSpec(shape, lambda c: (0, 0))

    columns = pl.BlockSpec((tokens, CB), lambda c: (0, c))
    return pl.pallas_call(
        combine_kernel,
        grid=(NCB,),
        in_specs=[
            whole(ROWS, tokens),
            whole(ROWS, 2 * D),
            whole(tokens, D),
            whole(tokens, 1),
            whole(tokens, EXPERTS),
            whole(tokens, EXPERTS),
            whole(tokens, D),
            whole(EXPERTS, D),
            whole(1, D),
            pl.BlockSpec((CB, D), lambda c: (c, 0)),
            columns,
            columns,
            columns,
            whole(tokens, DI),
            whole(tokens, D),
            ANYWHERE,
        ],
        out_specs=[
            whole(tokens, D),
            whole(tokens, D),
            whole(tokens, D),
            columns,
            columns,
            whole(16, D),
            pl.BlockSpec((16, 192, D), lambda c: (0, 2, 0)),
        ],
        out_shape=[
            shape_of(tokens, D, dtype=bf16),
            shape_of(tokens, D),
            shape_of(tokens, D, dtype=bf16),
            shape_of(tokens, DI),
            shape_of(tokens, DI, dtype=bf16),
            shape_of(16, D),
            shape_of(16, 576, D, dtype=bf16),
        ],
        input_output_aliases={15: 6},
        compiler_params=EXP_PARAMS,
        cost_estimate=lasting(12),
        name="combine",
    )(
        table, back, residual, gate, probs, hot, grad, router, gain, out_w, act, slope, my, gated, normed, held
    )


def other_grad_kernel(place_ref, cin_ref, next_ref, normed_ref, small_ref, low_ref, out_ref):
    for m in range(MICRO):
        low_ref[m * TOK : (m + 1) * TOK - 16, :] = cin_ref[m, : TOK - 16, :].astype(bf16)
        last = jnp.concatenate(
            [cin_ref[m, TOK - 16 : TOK - 8, :], cin_ref[m, TOK - 8 :, :] + next_ref[m]], axis=0
        )
        low_ref[(m + 1) * TOK - 16 : (m + 1) * TOK, :] = last.astype(bf16)
    owned_rows(1 - place_ref[1], normed_ref[...], low_ref, small_ref, out_ref)


def other_grad_call(place, cin, following, normed, small):
    vmem = pl.BlockSpec(memory_space=pltpu.VMEM)
    return pl.pallas_call(
        other_grad_kernel,
        in_specs=[pl.BlockSpec(memory_space=pltpu.SMEM)] + [vmem] * 4,
        out_specs=[vmem] * 2,
        out_shape=[
            shape_of(MICRO * TOK, DI, dtype=bf16),
            shape_of(512, DI, dtype=bf16),
        ],
        compiler_params=pltpu.CompilerParams(vmem_limit_bytes=48 * MIB),
        cost_estimate=lasting(6),
        name="other_grad",
    )(place, cin, following, normed, small)


def own_grad_kernel(place_ref, low_ref, normed_ref, small_ref, out_ref):
    owned_rows(place_ref[1], normed_ref[...], low_ref, small_ref, out_ref)


def own_grad_call(place, low, normed, small):
    vmem = pl.BlockSpec(memory_space=pltpu.VMEM)
    return pl.pallas_call(
        own_grad_kernel,
        in_specs=[pl.BlockSpec(memory_space=pltpu.SMEM)] + [vmem] * 3,
        out_specs=vmem,
        out_shape=shape_of(512, DI, dtype=bf16),
        compiler_params=pltpu.CompilerParams(vmem_limit_bytes=48 * MIB),
        cost_estimate=lasting(6),
        name="own_grad",
    )(place, low, normed, small)


def input_grad_kernel(
    cin_ref,
    branch_ref,
    in_c_ref,
    late_ref,
    x_ref,
    gain_ref,
    residual_ref,
    before_ref,
    out_ref,
):
    k = lax.broadcasted_iota(jnp.int32, (1, D), 1)
    grad = dot(cin_ref[...], in_c_ref[...], 1, 1)
    for h in range(2):
        grad += dot(
            branch_ref[:, h * D : (h + 1) * D], late_ref[:, 2 * h * D : (2 * h + 1) * D], 1, 1
        )
    scaled = split_dot(grad, picks(gathered_row(k, 6), D)) * gain_ref[...]
    x = x_ref[...]
    scale = lax.rsqrt(jnp.mean(x * x, axis=-1, keepdims=True) + EPSILON)
    unit = x * scale
    out_ref[...] = residual_ref[...] + scale * (
        scaled - unit * jnp.mean(scaled * unit, axis=-1, keepdims=True)
    )


def input_grad_call(*args):
    return pl.pallas_call(
        input_grad_kernel,
        in_specs=[pl.BlockSpec(memory_space=pltpu.VMEM)] * 7 + [ANYWHERE],
        out_shape=shape_of(MICRO * TOK, D),
        compiler_params=pltpu.CompilerParams(vmem_limit_bytes=56 * MIB),
        cost_estimate=lasting(20),
        name="input_grad",
    )(*args)


def shares_kernel(place_ref, big_ref, before_ref, own_ref, other_ref):
    k = lax.broadcasted_iota(jnp.int32, (1, 96), 1)
    piece, row = k // 24, k % 24
    chip = (place_ref[0] + jnp.where(piece == 1, 3, jnp.where(piece == 2, 1, piece - piece // 3))) % CHIPS
    for core, ref in ((place_ref[1], own_ref), (1 - place_ref[1], other_ref)):
        owner = 2 * chip + core
        source = jnp.where(row < 12, owner * 12 + row, 96 + row // 18 * 48 + owner * 6 + row % 6)
        ref[...] = dot(picks(source, 192), big_ref[...], 0, 0).astype(bf16)


def shares_call(place, big, before):
    return pl.pallas_call(
        shares_kernel,
        grid=(1,),
        in_specs=[
            pl.BlockSpec(memory_space=pltpu.SMEM),
            pl.BlockSpec((192, D), lambda j: (2, 0)),
            ANYWHERE,
        ],
        out_specs=[pl.BlockSpec((96, D), lambda j: (0, 0))] * 2,
        out_shape=[shape_of(96, D, dtype=bf16)] * 2,
        compiler_params=EXP_PARAMS,
        cost_estimate=lasting(2),
        name="shares",
    )(place, big, before)


def expert_out_kernel(big_ref, before_ref, up_ref, down_ref):
    for j in range(NFB):
        up_ref[:, j * FB : (j + 1) * FB] = big_ref[j * 48 : (j + 1) * 48, :].astype(f32)
    down_ref[...] = big_ref[192:384, :].astype(f32)


def expert_out_call(big, before):
    return pl.pallas_call(
        expert_out_kernel,
        grid=(1,),
        in_specs=[pl.BlockSpec((384, D), lambda j: (0, 0)), ANYWHERE],
        out_specs=[
            pl.BlockSpec((48, FF), lambda j: (0, 0)),
            pl.BlockSpec((192, D), lambda j: (0, 0)),
        ],
        out_shape=[shape_of(48, FF), shape_of(192, D)],
        compiler_params=EXP_PARAMS,
        cost_estimate=lasting(2),
        name="expert_out",
    )(big, before)


def finish_kernel(
    total_ref,
    rest_ref,
    in_ref,
    gain_ref,
    before_ref,
    grad_in_ref,
    out_ref,
    norm_ref,
    state_ref,
    step_ref,
    decay_ref,
    conv_ref,
    conv_bias_ref,
    step_bias_ref,
    skip_ref,
    moe_ref,
    router_ref,
):
    total = jnp.sum(total_ref[...].astype(f32), axis=0)
    rest = rest_ref[...].astype(f32)
    out_ref[...] = rest[:12]
    grad_in_ref[:, :DI] = total[:6]
    grad_in_ref[:, DI : DI + D] = rest[12:18]
    grad_in_ref[:, DI + D :] = rest[18:24]
    part = jnp.sum(in_ref[...].astype(f32) * grad_in_ref[...], axis=1, keepdims=True)
    part = jnp.concatenate([jnp.broadcast_to(part, (6, LANES)), jnp.zeros((2, LANES), f32)], axis=0)
    norm_ref[...] = part.T[:1, :6] / gain_ref[...].astype(f32)
    rows = jnp.concatenate(
        [total[6 + c // 6 : 7 + c // 6, c % 6 * 160 : c % 6 * 160 + 160] for c in range(12)]
        + [jnp.zeros((4, 160), f32)],
        axis=0,
    )
    state_ref[...] = rows[:12, 72:152]
    turned = rows.T[:, :12]
    step_ref[...] = turned[:48]
    decay_ref[...] = turned[48:64]
    step_bias_ref[...] = turned[64:65]
    conv_ref[...] = turned[152:156]
    conv_bias_ref[...] = turned[156:157]
    skip_ref[...] = turned[65:66]
    wide = jnp.concatenate(
        [total[6:7, 960 + 16 * c : 976 + 16 * c] for c in range(6)] + [jnp.zeros((2, 16), f32)], axis=0
    )
    router_ref[...] = wide[:6, 1:9]
    moe_ref[...] = wide.T[:1, :6]


def finish_call(total, rest, in_proj, gain, before):
    return pl.pallas_call(
        finish_kernel,
        in_specs=[pl.BlockSpec(memory_space=pltpu.VMEM)] * 4 + [ANYWHERE],
        out_shape=[
            shape_of(6, 2 * DI),
            shape_of(12, D),
            shape_of(1, 6),
            shape_of(12, 80),
            shape_of(RANK, 12),
            shape_of(STATE, 12),
            shape_of(CONV, 12),
            shape_of(1, 12),
            shape_of(1, 12),
            shape_of(1, 12),
            shape_of(1, 6),
            shape_of(6, EXPERTS),
        ],
        compiler_params=pltpu.CompilerParams(vmem_limit_bytes=32 * MIB),
        cost_estimate=lasting(3),
        name="finish",
    )(total, rest, in_proj, gain, before)


def swap(v, axis):
    return lax.all_to_all(v, axis, 0, 0, tiled=True)


def spread(v, axis):
    n = lax.axis_size(axis) if isinstance(axis, str) else 128
    return swap(jnp.broadcast_to(v[None], (n,) + v.shape), axis)


def tied(*values):
    return lax.optimization_barrier(values)


CORE_SWAP = [(i, i ^ 1) for i in range(8)]
HOPS = (1, -1, 2)


def along_z(v, by):
    return lax.ppermute(
        v, "fsdp", [(2 * z + c, 2 * ((z + by) % CHIPS) + c) for z in range(CHIPS) for c in range(2)]
    )


def cores_total(own, other):
    return (own.astype(f32) + lax.ppermute(other, "fsdp", CORE_SWAP).astype(f32)).astype(bf16)


def chips_total(parts):
    parts = parts.reshape(CHIPS, parts.shape[0] // CHIPS, parts.shape[1])
    parts = [parts[0]] + [along_z(parts[i + 1], -by) for i, by in enumerate(HOPS)]
    return sum(p.astype(f32) for p in parts).astype(bf16)


def on_device(
    block_input,
    routes,
    cotangent,
    in_proj,
    conv_weight,
    conv_bias,
    state_proj,
    step_proj,
    step_bias,
    decay_log,
    skip_gain,
    out_proj,
    norm_gain,
    moe_gain,
    router,
    expert_up,
    expert_down,
):
    T = TOK
    place = lax.axis_index("fsdp").astype(jnp.int32)
    place = jnp.stack([place // 2, place % 2])
    small = jnp.concatenate(
        [
            state_proj,
            step_proj.T,
            decay_log.T,
            conv_weight.T,
            conv_bias[:, None],
            step_bias[:, None],
            skip_gain[:, None],
            jnp.zeros((12, 1), bf16),
        ],
        axis=1,
    ).reshape(1, 12 * WEIGHT_ROWS)
    wide = jnp.concatenate([norm_gain[:, None], moe_gain[:, None], router], axis=1)
    packed = jnp.concatenate([small, wide.reshape(1, 60), jnp.zeros((1, 1188), bf16)], axis=1)
    rows_c = spread(in_proj[:, :DI], "seq").reshape(96, DI)
    rows_late = jnp.concatenate(
        [in_proj[:, DI : DI + D], out_proj[:6], in_proj[:, DI + D :], out_proj[6:]], axis=1
    )
    rows_late = jnp.concatenate([rows_late, packed, jnp.zeros((1, 2 * DI), bf16)], axis=0)
    rows_c, rows_late = tied(rows_c, rows_late)
    in_c = lax.all_gather(rows_c, "fsdp", axis=0, tiled=True)
    rows_late = spread(rows_late, "seq")
    packed = swap(jnp.broadcast_to(rows_late[None, :, 6, :2048], (8, 16, 2048)), "fsdp")
    packed = packed.transpose(1, 0, 2).reshape(DEVICES, 2048)
    late = lax.all_gather(rows_late[:, :6].reshape(96, 2 * DI), "fsdp", axis=0, tiled=True)
    up_rows = expert_up[0].reshape(48, NFB, FB).transpose(1, 0, 2).reshape(192, FB)
    big = jnp.concatenate([up_rows, expert_down[0]], axis=0)

    weights = packed[:, : 12 * WEIGHT_ROWS].reshape(DI, WEIGHT_ROWS).T
    wide = packed[:, 12 * WEIGHT_ROWS : 12 * WEIGHT_ROWS + 60].reshape(D, 10).T
    norm_g, moe_g, router_w = wide[0:1].astype(f32), wide[1:2].astype(f32), wide[2:]

    x_tail = lax.ppermute(block_input[:, T - CONV + 1 :], ALL, [(i, i + 1) for i in range(127)])
    x_head = jnp.concatenate(
        [jnp.zeros((MICRO, HEAD - CONV + 1, D), bf16), x_tail, block_input], axis=1
    )
    normed_nat, normed_in, conv_in, conv, state_in, step_low, step, sig = front_call(
        x_head, norm_g, in_c, weights
    )
    conv_in, big = tied(conv_in, big)
    big = lax.all_gather(big, "seq", axis=0, tiled=False)
    x = block_input.reshape(MICRO * T, D).astype(f32)
    ends = end_state(step, conv, state_in, weights)
    pair = swap(ends, ALL)
    gate_act, gate_slope, out_w = gate_call(normed_in, late, ends)
    start = prefix(pair, pair, False, out_w)
    start = swap(start, ALL)
    one_hot_i = (
        routes.reshape(MICRO, T, 1) == lax.broadcasted_iota(jnp.int32, (MICRO, T, EXPERTS), 2)
    ).astype(jnp.int32)
    slot = jnp.sum((jnp.cumsum(one_hot_i, axis=1) - 1) * one_hot_i, axis=2)
    micro = lax.broadcasted_iota(jnp.int32, (MICRO, T), 0)
    position = (routes.reshape(MICRO, T) * (MICRO * CAP) + micro * CAP + slot).reshape(
        1, MICRO * T
    )
    table = (lax.broadcasted_iota(jnp.int32, (ROWS, MICRO * T), 0) == position).astype(bf16)
    one_hot = one_hot_i.reshape(MICRO * T, EXPERTS).astype(f32)
    grad_out = cotangent.reshape(MICRO * T, D).astype(f32)

    mixed_y, gated = scan(step, conv, state_in, weights, start, gate_act.reshape(MICRO, T, DI))
    gated = gated.reshape(MICRO * T, DI)
    residual, expert_gate, probs, sent = dispatch_call(
        gated,
        out_w,
        block_input.reshape(MICRO * T, D),
        moe_g,
        router_w,
        one_hot,
        table,
        cotangent.reshape(MICRO * T, D),
    )
    ah = history(step, conv, state_in, weights, start, sent)
    sent = swap(sent, "fsdp")
    hidden, grad_pre, back = expert_call(sent, big, ah)
    back = swap(back, "fsdp")
    grad_experts = expert_grad_call(sent, hidden, grad_pre)
    mixed, grad_residual, grad_mix, grad_y, grad_gate_branch, wide, grad_big = combine_call(
        table,
        back,
        residual,
        expert_gate,
        probs,
        one_hot,
        cotangent.reshape(MICRO * T, D),
        router_w,
        moe_g,
        out_w,
        gate_act,
        gate_slope,
        mixed_y.reshape(MICRO * T, DI),
        gated,
        normed_nat,
        grad_experts,
    )
    grad_y = grad_y.reshape(MICRO, T, DI)
    mu = end_adjoint(step, grad_y, state_in, weights)
    mus = swap(mu, ALL)
    grad_early = grad_big
    grad_big = lax.psum_scatter(
        grad_big.reshape(16 * 576, D), "seq", scatter_dimension=0, tiled=True
    )
    later = swap(prefix(pair, mus, True, grad_early), ALL)
    wide = wide.astype(bf16).T.reshape(DEVICES, 1, 96)

    grad_first, grad_cin, grad_halo, grad_second = scan_back(
        step, sig, conv, grad_y, ah, state_in, weights, later, conv_in, step_low
    )
    grad_next = lax.ppermute(grad_halo, ALL, [(i + 1, i) for i in range(127)])
    smalls = jnp.concatenate(
        [grad_first[0] + grad_first[1], grad_second[0] + grad_second[1]], axis=0
    ).astype(bf16)
    smalls = smalls.T.reshape(DEVICES, 2, 960)
    wide = jnp.pad(wide, ((0, 0), (0, 1), (0, 480)))
    smalls = jnp.concatenate([smalls, wide], axis=2).reshape(2 * DEVICES, DI)
    grad_cin, other = other_grad_call(place, grad_cin, grad_next, normed_nat, smalls)
    total = cores_total(own_grad_call(place, grad_cin, normed_nat, smalls), other)
    operand = total
    total = lax.all_to_all(
        total.reshape(64, 8, DI),
        ALL,
        0,
        0,
        tiled=True,
        axis_index_groups=[list(range(c, DEVICES, 2)) for c in (0, 1)],
    )
    grad_input = input_grad_call(
        grad_cin, grad_gate_branch, in_c, late, x, norm_g, grad_residual, operand
    )
    own, other = shares_call(place, grad_big, grad_input)
    rest = cores_total(own, other)
    grad_up, grad_down = expert_out_call(grad_big, rest)
    rest = chips_total(rest)
    (
        grad_in,
        grad_out_proj,
        grad_norm,
        grad_state,
        grad_step,
        grad_decay,
        grad_conv_weight,
        grad_conv_bias,
        grad_step_bias,
        grad_skip,
        grad_moe,
        grad_router,
    ) = finish_call(total, rest, in_proj, norm_gain.reshape(1, 6), grad_up)
    return (
        mixed.reshape(MICRO, T, D),
        grad_input.reshape(MICRO, T, D),
        grad_in,
        grad_conv_weight,
        grad_conv_bias.reshape(12),
        grad_state,
        grad_step,
        grad_step_bias.reshape(12),
        grad_decay,
        grad_skip.reshape(12),
        grad_out_proj,
        grad_norm.reshape(6),
        grad_moe.reshape(6),
        grad_router,
        grad_up[None],
        grad_down[None],
    )


def solution(mesh):
    return jax.shard_map(
        on_device,
        mesh=mesh,
        in_specs=(
            P(None, ALL, None),
            P(None, ALL, None),
            P(None, ALL, None),
            P(ALL, None),
            P(None, ALL),
            P(ALL),
            P(ALL, None),
            P(None, ALL),
            P(ALL),
            P(None, ALL),
            P(ALL),
            P(ALL, None),
            P(ALL),
            P(ALL),
            P(ALL, None),
            P("fsdp", "seq", None),
            P("fsdp", "seq", None),
        ),
        out_specs=(
            P(None, ALL, None),
            P(None, ALL, None),
            P(ALL, None),
            P(None, ALL),
            P(ALL),
            P(ALL, None),
            P(None, ALL),
            P(ALL),
            P(None, ALL),
            P(ALL),
            P(ALL, None),
            P(ALL),
            P(ALL),
            P(ALL, None),
            P("fsdp", "seq", None),
            P("fsdp", "seq", None),
        ),
        check_vma=False,
    )
```
